256 devices in a mesh: orb: 16 (over z, core), slab: 16 (over y, x).
Axes of the slice: x: 4, y: 4, z: 8, core: 2. Of those that a mesh axis runs over, the one named last changes fastest.
Arguments:
- orbitals: float32 [16, 128, 48, 128], P('orb', 'slab'), may hold values from -6 to 6
- occupations: float32 [16], P('orb'), may hold values from 0.25 to 1
Outputs:
- exchange: float32 [16, 128, 48, 128], P('orb', 'slab')
The draws below stay inside these ranges and needn't reach their ends.
All inputs are finite; a program needn't handle non-finite values.
Results may differ from the reference program's by a relative error of at most 0.0003.
Values sent between devices are 32-bit elements; how exact they have to be, the bound alone decides.
A program may use at most 128 MiB of HBM per device.

```python
import math
import jax
import jax.numpy as jnp
from jax import lax

ORB_DEV = 1
NY = 48
NX = 128
CYCLES = 2
LEVELS = 3
SWEEPS = 6
ORBS = 16
NZ = 128
N_ORB = 16


def steps_of(own_key, dims, pieces, least, high):
    loudness = 1.0
    for position, blocks in pieces:
        steps = jax.random.uniform(jax.random.fold_in(jax.random.fold_in(own_key, 6), position), (blocks,), jnp.float32, least / len(pieces), high / len(pieces))
        loudness = loudness * jnp.repeat(jnp.exp(steps), dims[position] // blocks).reshape((-1,) + (1,) * (len(dims) - 1 - position))
    return loudness


def centred(stream_key, shape, spread, reach, split=(), held_as=jnp.bfloat16):
    drawn = jax.random.normal(stream_key, shape, jnp.float32) * spread
    if len(split) > 0:
        drawn = steps_of(stream_key, shape, split, -0.22, 0.18) * drawn
    return jnp.clip(drawn, min=-reach, max=reach).astype(held_as)


def setup_inputs(seed: int = 0) -> dict:
    key_list = jax.random.split(jax.random.key(seed), 3)
    return {
        "orbitals": centred(key_list[0], (ORBS, NZ, NY, NX), 1.0, 6.0, ((0, 16), (1, 16)), jnp.float32),
        "occupations": jnp.clip(jnp.exp(math.log(1.0) - 1.3862944 * jax.random.uniform(key_list[1], (ORBS,), jnp.float32) ** steps_of(key_list[1], (ORBS,), ((0, 16),), -0.2, 0.2)), 0.25, 1.0),
    }


screening = 0.001
relaxation = 0.8


def operate(values, inverse_step):
    padded = jnp.pad(values, ((0, 0), (1, 1), (0, 0), (0, 0)))
    beside = padded[:, 2:] + padded[:, :-2]
    beside = beside + jnp.roll(values, 1, 2) + jnp.roll(values, -1, 2)
    beside = beside + jnp.roll(values, 1, 3) + jnp.roll(values, -1, 3)
    return (6.0 * inverse_step + screening) * values - inverse_step * beside


def smooth(values, source, inverse_step):
    return values + relaxation * (source - operate(values, inverse_step)) / (6.0 * inverse_step + screening)


def restrict(values):
    shape = values.shape
    grouped = values.reshape(shape[0], shape[1] // 2, 2, shape[2] // 2, 2, shape[3] // 2, 2)
    return jnp.sum(grouped, axis=(2, 4, 6)) * 0.125


def prolong(values):
    return jnp.repeat(jnp.repeat(jnp.repeat(values, 2, 1), 2, 2), 2, 3)


def vcycle(values, source, level_index):
    inverse_step = 0.25 ** level_index
    if level_index == LEVELS:
        iterate = jnp.zeros_like(source)
        for sweep_index in range(SWEEPS):
            iterate = smooth(iterate, source, inverse_step)
        return iterate
    iterate = smooth(values, source, inverse_step)
    residual = source - operate(iterate, inverse_step)
    coarse_source = restrict(residual)
    correction = vcycle(jnp.zeros_like(coarse_source), coarse_source, level_index + 1)
    iterate = iterate + prolong(correction)
    return smooth(iterate, source, inverse_step)


def solve(source):
    iterate = jnp.zeros_like(source)
    for cycle_index in range(CYCLES):
        iterate = vcycle(iterate, source, 0)
    return iterate


def reference(orbitals, occupations):
    def block_exchange(block_index):
        first_row = block_index * ORB_DEV
        left_row = ((block_index + N_ORB - 1) % N_ORB) * ORB_DEV
        right_row = ((block_index + 1) % N_ORB) * ORB_DEV
        own_orbs = lax.dynamic_slice_in_dim(orbitals, first_row, ORB_DEV, 0)
        visiting = jnp.stack([lax.dynamic_slice_in_dim(orbitals, left_row, ORB_DEV, 0),
                              lax.dynamic_slice_in_dim(orbitals, right_row, ORB_DEV, 0)])
        weights = jnp.stack([lax.dynamic_slice_in_dim(occupations, left_row, ORB_DEV, 0),
                             lax.dynamic_slice_in_dim(occupations, right_row, ORB_DEV, 0)])
        density = own_orbs[None, :, None] * visiting[:, None, :]
        shape = density.shape
        potential = solve(density.reshape((2 * ORB_DEV * ORB_DEV,) + shape[3:])).reshape(shape)
        weighted = visiting * weights[:, :, None, None, None]
        return -jnp.sum(potential * weighted[:, None], axis=(0, 2))

    blocks = lax.map(block_exchange, jnp.arange(N_ORB, dtype=jnp.int32))
    return blocks.reshape(orbitals.shape)
```

```python
import functools

import jax
import jax.numpy as jnp
from jax import lax
from jax.experimental import pallas as pl
from jax.experimental.pallas import tpu as pltpu
from jax.sharding import PartitionSpec as P

MESH = pl.DeviceIdType.MESH

NZ, NY, NX = 128, 48, 128
SWEEPS = 6
screening = 0.001
relaxation = 0.8

STEP = [0.25**level for level in range(4)]
CENTRE = [6.0 * step + screening for step in STEP]
KEEP = 1.0 - relaxation
PULL = [relaxation / centre for centre in CENTRE]
SIDE = [pull * step for pull, step in zip(PULL, STEP)]

ROWS1 = 48
MSG = 16


def turn(value, by, axis):
    return pltpu.roll(value, by % value.shape[axis], axis)


def lanes(rows):
    return lax.broadcasted_iota(jnp.int32, (rows, 128), 1)


def in_plane(value, lane_step):
    return (turn(value, 1, 0) + turn(value, -1, 0)) + (turn(value, lane_step, 1) + turn(value, -lane_step, 1))


def swapped(value, bit):
    first = (lanes(value.shape[0]) & bit) == 0
    return jnp.where(first, turn(value, -bit, 1), turn(value, bit, 1))


def total(parts):
    parts = [part for part in parts if part is not None]
    while len(parts) > 1:
        parts = [a + b for a, b in zip(parts[::2], parts[1::2])] + parts[len(parts) // 2 * 2 :]
    return parts[0] if parts else None


def kernel(
    n_orb, n_slab,
    occ_ref, orb_ref, out_ref,
    own, right, occ_out, occ_in, f, v2, v, v1, pe1, f1, src1, e1, pe2, f1_out, f1_in, gather, e2,
    ret_out, ret_in,
    local_sem, orb_send, orb_recv, occ_sems, gat_send, gat_recv, f1_send, f1_recv, f_send, f_recv, ret_send, ret_recv,
):
    o, s = lax.axis_index("orb"), lax.axis_index("slab")
    right_orb, left_orb = lax.rem(o + 1, n_orb), lax.rem(o + n_orb - 1, n_orb)
    above, below = lax.rem(s + 1, n_slab), lax.rem(s + n_slab - 1, n_slab)
    odd = lax.rem(s, 2)

    def at_slab(index):
        return {"slab": index}

    def at_orb(index):
        return {"orb": index}

    mine = pltpu.make_async_copy(orb_ref.at[0], own, local_sem)
    mine.start()

    barrier = pltpu.get_barrier_semaphore()
    pl.semaphore_signal(barrier, inc=1, device_id=at_orb(left_orb), device_id_type=MESH)
    pl.semaphore_signal(barrier, inc=1, device_id=at_orb(right_orb), device_id_type=MESH)
    for k in range(1, n_slab):
        pl.semaphore_signal(barrier, inc=1, device_id=at_slab(lax.rem(s + k, n_slab)), device_id_type=MESH)

    occ_out[...] = jnp.full((8, 128), occ_ref[0], jnp.float32)
    for g in range(2):
        for slot in (0, 17):
            gather[pl.ds((g * 18 + slot) * MSG, MSG), :] = jnp.zeros((MSG, 128), jnp.float32)
    e2[...] = jnp.zeros_like(e2)
    src1[...] = jnp.zeros_like(src1)
    low = jnp.where(s > 0, 1.0, 0.0).astype(jnp.float32)
    high = jnp.where(s < n_slab - 1, 1.0, 0.0).astype(jnp.float32)

    def inside(plane, count):
        return low if plane < 0 else high if plane >= count else 1.0

    pl.semaphore_wait(barrier, n_slab + 1)

    halves = []
    for h in range(2):
        planes = pl.ds(4 * h, 4)
        halves.append(pltpu.make_async_remote_copy(
            orb_ref.at[0, planes], right.at[planes], orb_send.at[h], orb_recv.at[h],
            device_id=at_orb(left_orb), device_id_type=MESH))
        halves[-1].start()
    occ_copy = pltpu.make_async_remote_copy(
        occ_out, occ_in, occ_sems.at[0], occ_sems.at[1], device_id=at_orb(left_orb), device_id_type=MESH)
    occ_copy.start()

    mine.wait()
    for h in range(2):
        halves[h].wait_recv()
        for p in range(4 * h, 4 * h + 4):
            f[3 + p] = own[p] * right[p]

    pending = []

    def send(src, dst, send_sem, recv_sem, device):
        copy = pltpu.make_async_remote_copy(src, dst, send_sem, recv_sem, device_id=device, device_id_type=MESH)
        copy.start()
        pending.append(copy)
        return copy

    def restricted(pair, beyond, source, centre, side, bit):
        beyond = total([part for plane in beyond for part in plane[:2]])
        terms = []
        if pair:
            even, odd_, before, after = [total([plane[i] for plane in pair]) for i in range(4)]
            both = even + odd_
            terms.append(centre * both)
            around = total([both + both, before, after, turn(both, bit, 1), turn(both, -bit, 1), beyond])
        else:
            around = beyond
        terms.append(side * around)
        terms += [part for plane in source for part in plane]
        mean = total(terms)
        return 0.125 * (mean + swapped(mean, bit))

    def fine_rows(ref, plane):
        even, odd_ = ref[plane, pl.ds(0, 24, stride=2), :], ref[plane, pl.ds(1, 24, stride=2), :]
        return even, odd_, turn(odd_, 1, 0), turn(even, -1, 0)

    def put_src1(slot, value):
        src1[slot, 8:32, :] = value
        src1[slot, 7:8, :] = value[23:24]
        src1[slot, 32:33, :] = value[0:1]

    def coarse_rows(slot):
        return [src1[slot, pl.ds(8 + start, MSG, stride=2), :] for start in (0, 1, -1, 2)]

    lane16 = lanes(MSG)
    place16 = (lane16 + 2 * odd) & 3

    def send_level2(g, have):
        parts = {}
        for d in range(-1, 3):
            pair = [coarse_rows(q + 1) for q in (2 * d, 2 * d + 1) if q in have]
            beyond = [coarse_rows(q + 1) for q in (2 * d - 1, 2 * d + 2) if q in have]
            parts[d] = restricted(pair, beyond, [], KEEP, SIDE[1], 2)
        packed = jnp.where(place16 == 0, parts[0], jnp.where(place16 == 1, parts[1], jnp.where(place16 == 2, parts[2], parts[-1])))
        base = g * 18 * MSG
        slot = pl.ds(pl.multiple_of(base + (s + 1) * MSG, MSG), MSG)
        gather[slot, :] = packed
        for k in range(1, n_slab):
            pltpu.make_async_remote_copy(
                gather.at[slot], gather.at[slot], gat_send.at[g], gat_recv.at[g],
                device_id=at_slab(lax.rem(s + k, n_slab)), device_id_type=MESH).start()

    def gathered(g):
        most = gather.at[pl.ds(g * 18 * MSG, (n_slab - 1) * MSG)]
        return pltpu.make_async_remote_copy(
            most, most, gat_send.at[g], gat_recv.at[g], device_id=at_slab(above), device_id_type=MESH)

    row8 = lax.broadcasted_iota(jnp.int32, (8, 128), 0)
    lane8 = lanes(8)
    first_row, last_row = row8 == 0, row8 == 7

    def level2_sides(u):
        result = []
        for y in range(12):
            here = u[y]
            up = jnp.where(last_row, 0.0, turn(turn(here, 3, 1), -1, 0))
            down = jnp.where(first_row, 0.0, turn(turn(here, -3, 1), 1, 0))
            up = jnp.where((lane8 & 3) == 3, up, turn(here, -1, 1))
            down = jnp.where((lane8 & 3) == 0, down, turn(here, 1, 1))
            x = turn(here, 4, 1) + turn(here, -4, 1)
            result.append(total([u[(y + 1) % 12], u[(y + 11) % 12], up, down, x]))
        return result

    def level3_sides(u):
        result = []
        lower = (lane8 & 2) == 0
        for y in range(6):
            here = u[y]
            a, b = turn(here, -2, 1), turn(here, 2, 1)
            far = jnp.where(lower, jnp.where(first_row, 0.0, turn(a, 1, 0)), jnp.where(last_row, 0.0, turn(b, -1, 0)))
            x = turn(here, 8, 1) + turn(here, -8, 1)
            result.append(total([u[(y + 1) % 6], u[(y + 5) % 6], jnp.where(lower, a, b), far, x]))
        return result

    def solve_level2(g):
        base = g * 18 * MSG + MSG
        source = []
        for y in range(12):
            at = [gather[pl.ds(base + y + MSG * k, 8, stride=2 * MSG), :] for k in (0, 1)]
            after = gather[pl.ds(base + y + MSG * 2, 8, stride=2 * MSG), :]
            before = gather[pl.ds(base + y - MSG, 8, stride=2 * MSG), :]
            source.append(jnp.where((lane8 & 3) == 3, after, at[0]) + jnp.where((lane8 & 3) == 0, before, at[1]))
        sides = level2_sides(source)
        residual = [KEEP * a + SIDE[2] * b for a, b in zip(source, sides)]
        source3 = []
        for y in range(6):
            pair = residual[2 * y] + residual[2 * y + 1]
            pair = pair + swapped(pair, 1)
            source3.append(0.125 * (pair + swapped(pair, 4)))
        pull = [PULL[3] * a for a in source3]
        iterate = pull
        for _ in range(SWEEPS - 1):
            sides = level3_sides(iterate)
            iterate = [KEEP * a + b + SIDE[3] * c for a, b, c in zip(iterate, pull, sides)]
        pull = [PULL[2] * a for a in source]
        u = [a + iterate[y // 2] for y, a in enumerate(pull)]
        sides = level2_sides(u)
        for y in range(12):
            e2[24 * y + 8 : 24 * y + 16, :] = KEEP * u[y] + pull[y] + SIDE[2] * sides[y]

    def spread_level2(ds):
        row = (s + 1) // 2 - 1
        a = e2[pl.ds(8 + row, MSG, stride=24), :]
        b = e2[pl.ds(9 + row, MSG, stride=24), :]
        middle = jnp.where(odd == 1, a, b)
        for d in ds:
            value = jnp.where(place16 == d % 4, a if d < 0 else middle if d < 2 else b, 0.0)
            value = value + swapped(value, 1)
            value = value + swapped(value, 2)
            pe2[d + 2, pl.ds(0, MSG, stride=2), :] = value
            pe2[d + 2, pl.ds(1, MSG, stride=2), :] = value

    even24 = (lanes(24) & 1) == 0

    def packed(a, b):
        return jnp.where(even24, a, b)

    def unpacked(value):
        return jnp.where(even24, value, turn(value, 1, 1)), jnp.where(even24, turn(value, -1, 1), value)

    def correct_level1(reach):
        u = {}
        for q in range(-reach - 1, 5 + reach):
            u[q] = PULL[1] * f1[q + 3] + pe2[q // 2 + 2, 0:24, :]
        for q in range(-reach, 4 + reach):
            sides = total([u[q - 1], u[q + 1], in_plane(u[q], 2)])
            value = KEEP * u[q] + PULL[1] * f1[q + 3] + (SIDE[1] * inside(q, 4)) * sides
            pe1[q + 2, pl.ds(0, 24, stride=2), :] = value
            pe1[q + 2, pl.ds(1, 24, stride=2), :] = value

    for q in range(-1, 5):
        pair = [fine_rows(f, p + 3) for p in (2 * q, 2 * q + 1) if 0 <= p < 8]
        beyond = [fine_rows(f, p + 3) for p in (2 * q - 1, 2 * q + 2) if 0 <= p < 8]
        part = restricted(pair, beyond, [], KEEP, SIDE[0] * inside(q, 4), 1)
        put_src1(q + 1, part)
    send_level2(0, range(-1, 5))
    parts = [src1[q + 1, 8:32, :] for q in range(-1, 5)]
    for i in range(2):
        f1_out[0, i] = packed(parts[2 * i], parts[2 * i + 1])
        f1_out[1, i] = packed(parts[2 * i + 2], parts[2 * i + 3])
    for side, device in ((0, below), (1, above)):
        send(f1_out.at[side, pl.ds(0, 2)], f1_in.at[side, pl.ds(0, 2)], f1_send.at[side], f1_recv.at[side], at_slab(device))
    send(f.at[pl.ds(3, 3)], f.at[pl.ds(11, 3)], f_send.at[0], f_recv.at[0], at_slab(below))
    send(f.at[pl.ds(8, 3)], f.at[pl.ds(0, 3)], f_send.at[1], f_recv.at[1], at_slab(above))

    gathered(0).wait_recv()
    solve_level2(0)
    spread_level2(range(-2, 4))
    pending[0].wait_recv()
    pending[1].wait_recv()
    under = [low * plane for i in range(2) for plane in unpacked(f1_in[1, i])]
    over = [high * plane for i in range(2) for plane in unpacked(f1_in[0, i])]
    f1[0] = under[0]
    f1[1] = under[1]
    f1[2] = under[2] + parts[0]
    f1[3] = under[3] + parts[1]
    f1[4] = parts[2]
    f1[5] = parts[3]
    f1[6] = parts[4] + over[0]
    f1[7] = parts[5] + over[1]
    f1[8] = over[2]
    f1[9] = over[3]
    correct_level1(2)
    pending[2].wait_recv()
    pending[3].wait_recv()
    for p in range(-3, 11):
        v2[p + 3] = (PULL[0] * inside(p, 8)) * f[p + 3] + pe1[p // 2 + 2]

    def smooth(ref, slot, plane):
        here = ref[slot]
        sides = total([ref[slot - 1], ref[slot + 1], in_plane(here, 1)])
        flag = inside(plane, 8)
        return KEEP * here + (PULL[0] * flag) * f[plane + 3] + (SIDE[0] * flag) * sides

    for p in range(-2, 10):
        v[p + 2] = smooth(v2, p + 3, p)

    for p in range(-1, 9):
        v1[p + 1] = smooth(v, p + 2, p)
    for q in range(4):
        pair = [fine_rows(v1, p + 1) for p in (2 * q, 2 * q + 1)]
        beyond = [fine_rows(v1, p + 1) for p in (2 * q - 1, 2 * q + 2)]
        source = [fine_rows(f, p + 3)[:2] for p in (2 * q, 2 * q + 1)]
        put_src1(q + 1, restricted(pair, beyond, source, -CENTRE[0], STEP[0], 1))
    send_level2(1, range(4))
    parts = [src1[q + 1, 8:32, :] for q in range(4)]
    for side, device in ((0, below), (1, above)):
        f1_out[side, 2] = packed(parts[2 * side], parts[2 * side + 1])
        send(f1_out.at[side, pl.ds(2, 1)], f1_in.at[side, pl.ds(2, 1)], f1_send.at[side + 2], f1_recv.at[side + 2], at_slab(device))
    for q in range(4):
        f1[q + 3] = parts[q]
    gathered(1).wait_recv()
    solve_level2(1)
    spread_level2(range(-1, 3))
    pending[4].wait_recv()
    pending[5].wait_recv()
    under, over = unpacked(f1_in[1, 2]), unpacked(f1_in[0, 2])
    for i in range(2):
        f1[1 + i] = low * under[i]
        f1[7 + i] = high * over[i]
    correct_level1(1)
    for p in range(-1, 9):
        v2[p + 3] = v1[p + 1] + pe1[p // 2 + 2]

    occ_copy.wait_recv()
    mine_occ, right_occ = -occ_out[0:1, :], -occ_in[0:1, :]
    for h in range(4):
        for p in range(2 * h, 2 * h + 2):
            potential = smooth(v2, p + 3, p)
            ret_out[p] = (potential * mine_occ) * own[p]
            v[p] = (potential * right_occ) * right[p]
        planes = pl.ds(2 * h, 2)
        send(ret_out.at[planes], ret_in.at[planes], ret_send.at[h], ret_recv.at[h], at_orb(right_orb))
    for h in range(4):
        pending[6 + h].wait_recv()
        for p in range(2 * h, 2 * h + 2):
            out_ref[0, p] = v[p] + ret_in[p]

    for copy in halves:
        copy.wait_send()
    occ_copy.wait_send()
    for copy in pending:
        copy.wait_send()
    for g in range(2):
        gathered(g).wait_send()


def on_device(n_orb, n_slab, orbitals, occupations):
    vmem, dma = pltpu.VMEM, pltpu.SemaphoreType.DMA
    f32 = jnp.float32

    def fine(planes):
        return vmem((planes, NY, NX), f32)

    return pl.pallas_call(
        functools.partial(kernel, n_orb, n_slab),
        out_shape=jax.ShapeDtypeStruct(orbitals.shape, f32),
        in_specs=[pl.BlockSpec(memory_space=pltpu.SMEM), pl.BlockSpec(memory_space=pl.ANY)],
        out_specs=pl.BlockSpec(memory_space=pltpu.VMEM),
        scratch_shapes=[
            fine(8), fine(8), vmem((8, 128), f32), vmem((8, 128), f32),
            fine(14), fine(14), fine(12), fine(10), fine(8),
            vmem((10, 24, 128), f32), vmem((6, ROWS1, 128), f32), vmem((8, 24, 128), f32), vmem((6, 32, 128), f32),
            vmem((2, 3, 24, 128), f32), vmem((2, 3, 24, 128), f32),
            vmem((2 * 18 * MSG, 128), f32), vmem((24 * MSG, 128), f32),
            fine(8), fine(8),
            dma, dma((2,)), dma((2,)), dma((2,)), dma((2,)), dma((2,)), dma((4,)), dma((4,)), dma((2,)), dma((2,)), dma((4,)), dma((4,)),
        ],
        compiler_params=pltpu.CompilerParams(collective_id=0, has_side_effects=True, vmem_limit_bytes=32 * 2**20),
    )(occupations, orbitals)


def solution(mesh):
    return jax.shard_map(
        functools.partial(on_device, mesh.shape["orb"], mesh.shape["slab"]),
        mesh=mesh,
        in_specs=(P("orb", "slab", None, None), P("orb")),
        out_specs=P("orb", "slab", None, None),
        check_vma=False,
    )
```

```python
import functools

import jax
import jax.numpy as jnp
import numpy as np
from jax import lax
from jax.experimental import pallas as pl
from jax.experimental.pallas import tpu as pltpu
from jax.sharding import PartitionSpec as P

MESH = pl.DeviceIdType.MESH

NZ, NY, NX = 128, 48, 128
SWEEPS = 6
screening = 0.001
relaxation = 0.8

STEP = [0.25**level for level in range(4)]
CENTRE = [6.0 * step + screening for step in STEP]
KEEP = 1.0 - relaxation
PULL = [relaxation / centre for centre in CENTRE]
SIDE = [pull * step for pull, step in zip(PULL, STEP)]

ROWS1 = 48
MSG = 16
MSG2 = 24


def response_weights():
    def sides(u):
        padded = np.pad(u, ((0, 0), (1, 1), (0, 0), (0, 0)))
        return padded[:, 2:] + padded[:, :-2] + sum(np.roll(u, by, axis) for by in (1, -1) for axis in (2, 3))

    def smoothed(u, level):
        return KEEP * u + SIDE[level] * sides(u)

    def mean(u):
        b, z, y, x = u.shape
        return u.reshape(b, z // 2, 2, y // 2, 2, x // 2, 2).mean((2, 4, 6))

    def spread(u):
        return u.repeat(2, 1).repeat(2, 2).repeat(2, 3)

    unit = np.zeros((8, 8, 6, 6))
    for z in range(8):
        unit[z, z, 0, 0] = 1.0
    u = spread(smoothed(spread(unit), 1))
    u = smoothed(smoothed(u, 0), 0)
    u = mean(STEP[0] * sides(u) - CENTRE[0] * u)
    u = mean(smoothed(u, 1))
    weights = np.zeros((8, 5, 3, 3))
    for z in range(8):
        for dz in range(-2, 3):
            if 0 <= z + dz < 8:
                weights[z, dz + 2] = u[z, z + dz, :3, :3]
    return weights


def turn(value, by, axis):
    return pltpu.roll(value, by % value.shape[axis], axis)


def lanes(rows):
    return lax.broadcasted_iota(jnp.int32, (rows, 128), 1)


def in_plane(value, lane_step):
    return (turn(value, 1, 0) + turn(value, -1, 0)) + (turn(value, lane_step, 1) + turn(value, -lane_step, 1))


def swapped(value, bit):
    first = (lanes(value.shape[0]) & bit) == 0
    return jnp.where(first, turn(value, -bit, 1), turn(value, bit, 1))


def total(parts):
    parts = [part for part in parts if part is not None]
    while len(parts) > 1:
        parts = [a + b for a, b in zip(parts[::2], parts[1::2])] + parts[len(parts) // 2 * 2 :]
    return parts[0] if parts else None


def kernel(
    n_orb, n_slab,
    occ_ref, orb_ref, out_ref,
    left, occ_out, occ_in, f, v2, v, v1, pe1, f1, src1, pe2, f1_out, f1_in, msg2, gather, gather2, e2,
    ret_out, ret_in,
    orb_send, orb_recv, occ_sems, gat_send, gat_recv, f1_send, f1_recv, f_send, f_recv, ret_send, ret_recv,
):
    o, s = lax.axis_index("orb"), lax.axis_index("slab")
    prev_orb, next_orb = lax.rem(o + n_orb - 1, n_orb), lax.rem(o + 1, n_orb)
    above, below = lax.rem(s + 1, n_slab), lax.rem(s + n_slab - 1, n_slab)
    odd = lax.rem(s, 2)

    def at_slab(index):
        return {"slab": index}

    def at_orb(index):
        return {"orb": index}

    own = orb_ref.at[0]
    peers = sorted(((x, y) for x in range(4) for y in range(4) if x or y), key=lambda d: -min(d[0], 4 - d[0]) - min(d[1], 4 - d[1]))
    peers = [4 * lax.rem(s // 4 + y, 4) + lax.rem(s + x, 4) for x, y in peers]

    barrier = pltpu.get_barrier_semaphore()
    pl.semaphore_signal(barrier, inc=1, device_id=at_orb(next_orb), device_id_type=MESH)
    pl.semaphore_signal(barrier, inc=1, device_id=at_orb(prev_orb), device_id_type=MESH)
    for peer in peers:
        pl.semaphore_signal(barrier, inc=1, device_id=at_slab(peer), device_id_type=MESH)

    occ_out[...] = jnp.full((8, 128), occ_ref[0], jnp.float32)
    for slot in (0, 17):
        gather[pl.ds(slot * MSG, MSG), :] = jnp.zeros((MSG, 128), jnp.float32)
    for slot in (0, 18):
        gather2[pl.ds(slot * MSG2, 2 * MSG2), :] = jnp.zeros((2 * MSG2, 128), jnp.float32)
    e2[...] = jnp.zeros_like(e2)
    src1[...] = jnp.zeros_like(src1)
    low = jnp.where(s > 0, 1.0, 0.0).astype(jnp.float32)
    high = jnp.where(s < n_slab - 1, 1.0, 0.0).astype(jnp.float32)
    low2 = jnp.where(s > 1, 1.0, 0.0).astype(jnp.float32)
    high2 = jnp.where(s < n_slab - 2, 1.0, 0.0).astype(jnp.float32)

    def inside(plane, count):
        return low if plane < 0 else high if plane >= count else 1.0

    pl.semaphore_wait(barrier, n_slab + 1)

    halves = []
    for h in range(2):
        planes = pl.ds(4 * h, 4)
        halves.append(pltpu.make_async_remote_copy(
            orb_ref.at[0, planes], left.at[planes], orb_send.at[h], orb_recv.at[h],
            device_id=at_orb(next_orb), device_id_type=MESH))
        halves[-1].start()
    occ_copy = pltpu.make_async_remote_copy(
        occ_out, occ_in, occ_sems.at[0], occ_sems.at[1], device_id=at_orb(next_orb), device_id_type=MESH)
    occ_copy.start()

    for h in range(2):
        halves[h].wait_recv()
        for p in range(4 * h, 4 * h + 4):
            f[7 + p] = own[p] * left[p]

    def remote(src, dst, send_sem, recv_sem, device):
        return pltpu.make_async_remote_copy(src, dst, send_sem, recv_sem, device_id=device, device_id_type=MESH)

    pending = []

    def send(src, dst, send_sem, recv_sem, device):
        copy = remote(src, dst, send_sem, recv_sem, device)
        copy.start()
        pending.append(copy)
        return copy

    def restricted(pair, beyond, source, centre, side, bit):
        beyond = total([part for plane in beyond for part in plane[:2]])
        terms = []
        if pair:
            even, odd_, before, after = [total([plane[i] for plane in pair]) for i in range(4)]
            both = even + odd_
            terms.append(centre * both)
            around = total([both + both, before, after, turn(both, bit, 1), turn(both, -bit, 1), beyond])
        else:
            around = beyond
        terms.append(side * around)
        terms += [part for plane in source for part in plane]
        mean = total(terms)
        return 0.125 * (mean + swapped(mean, bit))

    def fine_rows(ref, plane):
        even, odd_ = ref[plane, pl.ds(0, 24, stride=2), :], ref[plane, pl.ds(1, 24, stride=2), :]
        return even, odd_, turn(odd_, 1, 0), turn(even, -1, 0)

    def put_src1(slot, value):
        src1[slot, 8:32, :] = value
        src1[slot, 7:8, :] = value[23:24]
        src1[slot, 32:33, :] = value[0:1]

    def coarse_rows(slot):
        return [src1[slot, pl.ds(8 + start, MSG, stride=2), :] for start in (0, 1, -1, 2)]

    lane16 = lanes(MSG)
    place16 = (lane16 + 2 * odd) & 3

    def level2_parts(have, planes):
        parts = {}
        for d in planes:
            pair = [coarse_rows(q + 4) for q in (2 * d, 2 * d + 1) if q in have]
            beyond = [coarse_rows(q + 4) for q in (2 * d - 1, 2 * d + 2) if q in have]
            parts[d] = restricted(pair, beyond, [], KEEP, SIDE[1], 2)
        return parts

    def laid(parts, planes):
        by_place = {d % 4: parts[d] for d in planes}
        return jnp.where(place16 < 2, jnp.where(place16 == 0, by_place[0], by_place[1]), jnp.where(place16 == 2, by_place[2], by_place[3]))

    slot1 = pl.ds(pl.multiple_of((s + 1) * MSG, MSG), MSG)
    slot2 = pl.ds(pl.multiple_of((s + 2) * MSG2, MSG2), MSG2)

    def send_first(parts):
        gather[slot1, :] = laid(parts, range(-1, 3))
        for peer in peers:
            remote(gather.at[slot1], gather.at[slot1], gat_send.at[0], gat_recv.at[0], at_slab(peer)).start()

    def send_second(parts):
        msg2[0:12, :] = laid(parts, range(-1, 3))[0:12]
        msg2[12:24, :] = laid(parts, (-3, -2, 3, 4))[0:12]
        gather2[slot2, :] = msg2[...]
        for peer in peers:
            remote(msg2, gather2.at[slot2], gat_send.at[1], gat_recv.at[1], at_slab(peer)).start()

    def gathered(g):
        most = gather.at[pl.ds(0, (n_slab - 1) * MSG)] if g == 0 else gather2.at[pl.ds(0, (n_slab - 1) * MSG2)]
        return remote(most, most, gat_send.at[g], gat_recv.at[g], at_slab(above))

    row8 = lax.broadcasted_iota(jnp.int32, (8, 128), 0)
    lane8 = lanes(8)
    first_row, last_row = row8 == 0, row8 == 7

    def level2_sides(u):
        result = []
        for y in range(12):
            here = u[y]
            up = jnp.where(last_row, 0.0, turn(turn(here, 3, 1), -1, 0))
            down = jnp.where(first_row, 0.0, turn(turn(here, -3, 1), 1, 0))
            up = jnp.where((lane8 & 3) == 3, up, turn(here, -1, 1))
            down = jnp.where((lane8 & 3) == 0, down, turn(here, 1, 1))
            x = turn(here, 4, 1) + turn(here, -4, 1)
            result.append(total([u[(y + 1) % 12], u[(y + 11) % 12], up, down, x]))
        return result

    def level3_sides(u):
        result = []
        lower = (lane8 & 2) == 0
        for y in range(6):
            here = u[y]
            a, b = turn(here, -2, 1), turn(here, 2, 1)
            far = jnp.where(lower, jnp.where(first_row, 0.0, turn(a, 1, 0)), jnp.where(last_row, 0.0, turn(b, -1, 0)))
            x = turn(here, 8, 1) + turn(here, -8, 1)
            result.append(total([u[(y + 1) % 6], u[(y + 5) % 6], jnp.where(lower, a, b), far, x]))
        return result

    place8 = lane8 & 3

    def first_source():
        source = []
        for y in range(12):
            even, odd_, even_after, odd_before = [gather[pl.ds(MSG * k + y, 8, stride=2 * MSG), :] for k in (1, 2, 3, 0)]
            source.append(jnp.where(place8 == 3, even_after, even) + jnp.where(place8 == 0, odd_before, odd_))
        return source

    def second_source():
        source = []
        for y in range(12):
            even, odd_, even_after, odd_before = [gather2[pl.ds(MSG2 * k + y, 8, stride=2 * MSG2), :] for k in (2, 3, 4, 1)]
            near = jnp.where(place8 == 3, even_after, even) + jnp.where(place8 == 0, odd_before, odd_)
            even_before, even, even_after, odd_before, odd_, odd_after = [
                gather2[pl.ds(MSG2 * k + 12 + y, 8, stride=2 * MSG2), :] for k in (0, 2, 4, 1, 3, 5)]
            far = jnp.where(place8 == 0, even_before, jnp.where(place8 == 3, even, even_after))
            far = far + jnp.where(place8 == 0, odd_, jnp.where(place8 == 3, odd_after, odd_before))
            source.append(near + far)
        return source

    def response(u):
        weights = response_weights()
        plane = 4 * row8 + place8

        def weight(dz, dy, dx):
            inner = float(weights[4, dz + 2, dy, dx])
            value = inner
            for at, z in ((0, 0), (1, 1), (30, 6), (31, 7)):
                if abs(weights[z, dz + 2, dy, dx] - inner) > 1e-12:
                    value = jnp.where(plane == at, jnp.float32(weights[z, dz + 2, dy, dx]), value)
            return value

        x1 = [turn(a, 4, 1) + turn(a, -4, 1) for a in u]
        x2 = [turn(a, 8, 1) + turn(a, -8, 1) for a in u]

        def beside(a, y, by):
            return a[(y + by) % 12] + a[(y - by) % 12]

        groups = ((0, 0), (0, 1), (0, 2), (1, 1), (1, 2))
        by_dz = {dz: [weight(dz, *group) for group in groups] for dz in (-1, 0, 1)}
        two = [float(weights[4, 4, dy, dx]) for dy, dx in ((0, 0), (0, 1), (1, 1))]
        result = []
        for y in range(12):
            sums = [u[y], x1[y] + beside(u, y, 1), x2[y] + beside(u, y, 2), beside(x1, y, 1), beside(x2, y, 1) + beside(x1, y, 2)]
            here, up, down = [total([w * a for w, a in zip(by_dz[dz], sums)]) for dz in (0, -1, 1)]
            far = two[0] * sums[0] + two[1] * sums[1] + two[2] * sums[3]
            up = jnp.where(place8 == 3, jnp.where(last_row, 0.0, turn(turn(up, 3, 1), -1, 0)), turn(up, -1, 1))
            down = jnp.where(place8 == 0, jnp.where(first_row, 0.0, turn(turn(down, -3, 1), 1, 0)), turn(down, 1, 1))
            a, b = turn(far, 2, 1), turn(far, -2, 1)
            far = jnp.where(place8 >= 2, a + jnp.where(last_row, 0.0, turn(a, -1, 0)), b + jnp.where(first_row, 0.0, turn(b, 1, 0)))
            result.append(total([here, up, down, far]))
        return result

    def solve_level2(source):
        sides = level2_sides(source)
        residual = [KEEP * a + SIDE[2] * b for a, b in zip(source, sides)]
        source3 = []
        for y in range(6):
            pair = residual[2 * y] + residual[2 * y + 1]
            pair = pair + swapped(pair, 1)
            source3.append(0.125 * (pair + swapped(pair, 4)))
        pull = [PULL[3] * a for a in source3]
        iterate = pull
        for _ in range(SWEEPS - 1):
            sides = level3_sides(iterate)
            iterate = [KEEP * a + b + SIDE[3] * c for a, b, c in zip(iterate, pull, sides)]
        pull = [PULL[2] * a for a in source]
        u = [a + iterate[y // 2] for y, a in enumerate(pull)]
        sides = level2_sides(u)
        return [KEEP * a + b + SIDE[2] * c for a, b, c in zip(u, pull, sides)]

    def spread_level2(g, ds):
        row = 24 * 16 * g + 8 + s // 2
        a, b, c = [e2[pl.ds(row + by, MSG, stride=24), :] for by in (-1, 0, 1)]
        for d in ds:
            rows = a if d == -3 else jnp.where(odd == 1, b, a) if d < 0 else b if d < 2 else jnp.where(odd == 1, c, b) if d < 4 else c
            value = jnp.where(place16 == d % 4, rows, 0.0)
            value = value + swapped(value, 1)
            value = value + swapped(value, 2)
            pe2[g, d + 3, pl.ds(0, MSG, stride=2), :] = value
            pe2[g, d + 3, pl.ds(1, MSG, stride=2), :] = value

    even24 = (lanes(24) & 1) == 0

    def packed(a, b):
        return jnp.where(even24, a, b)

    def unpacked(value):
        return jnp.where(even24, value, turn(value, 1, 1)), jnp.where(even24, turn(value, -1, 1), value)

    def put_pe1(q, value):
        pe1[q + 4, pl.ds(0, 24, stride=2), :] = value
        pe1[q + 4, pl.ds(1, 24, stride=2), :] = value

    def correct_level1(g, reach):
        u = {}
        for q in range(-reach - 1, 5 + reach):
            u[q] = PULL[1] * f1[q + 5] + pe2[g, q // 2 + 3, 0:24, :]
        for q in range(-reach, 4 + reach):
            sides = total([u[q - 1], u[q + 1], in_plane(u[q], 2)])
            put_pe1(q, KEEP * u[q] + PULL[1] * f1[q + 5] + (SIDE[1] * inside(q, 4)) * sides)

    def smooth(ref, first, planes, plane, source):
        flag = inside(plane, 8)
        near = [ref[p - first] for p in (plane - 1, plane + 1) if p in planes]
        terms = []
        if plane in planes:
            here = ref[plane - first]
            near.append(in_plane(here, 1))
            terms.append(KEEP * here)
        if plane in source:
            terms.append((PULL[0] * flag) * f[plane + 7])
        return total(terms + [(SIDE[0] * flag) * total(near)])

    def residual_mean(q, planes, source):
        pair = [fine_rows(v1, p + 6) for p in (2 * q, 2 * q + 1) if p in planes]
        beyond = [fine_rows(v1, p + 6) for p in (2 * q - 1, 2 * q + 2) if p in planes]
        rows = [fine_rows(f, p + 7)[:2] for p in (2 * q, 2 * q + 1) if p in source]
        return restricted(pair, beyond, rows, -CENTRE[0], STEP[0], 1)

    slab = range(8)
    for q in range(-1, 5):
        pair = [fine_rows(f, p + 7) for p in (2 * q, 2 * q + 1) if p in slab]
        beyond = [fine_rows(f, p + 7) for p in (2 * q - 1, 2 * q + 2) if p in slab]
        put_src1(q + 4, restricted(pair, beyond, [], KEEP, SIDE[0] * inside(q, 4), 1))
    send_first(level2_parts(range(-1, 5), range(-1, 3)))
    parts = {q: src1[q + 4, 8:32, :] for q in range(-1, 5)}
    for i in range(3):
        f1_out[i] = packed(parts[2 * i - 1], parts[2 * i])
    below2, above2 = lax.rem(s + n_slab - 2, n_slab), lax.rem(s + 2, n_slab)
    send(f1_out, f1_in.at[pl.ds(3, 3)], f1_send.at[0], f1_recv.at[0], at_slab(below))
    send(f1_out, f1_in.at[pl.ds(0, 3)], f1_send.at[1], f1_recv.at[1], at_slab(above))
    send(f1_out.at[pl.ds(0, 1)], f1_in.at[pl.ds(7, 1)], f1_send.at[2], f1_recv.at[2], at_slab(below2))
    send(f1_out.at[pl.ds(2, 1)], f1_in.at[pl.ds(6, 1)], f1_send.at[3], f1_recv.at[3], at_slab(above2))
    pulled = {q: PULL[1] * parts[q] for q in parts}
    for q in range(-2, 6):
        near = [pulled.get(q - 1), pulled.get(q + 1)]
        terms = []
        if q in parts:
            near.append(in_plane(pulled[q], 2))
            terms = [(KEEP + 1.0) * pulled[q]]
        put_pe1(q, total(terms + [(SIDE[1] * inside(q, 4)) * total(near)]))
    for p in range(-4, 12):
        v2[p + 7] = PULL[0] * f[p + 7] + pe1[p // 2 + 4] if p in slab else pe1[p // 2 + 4]
    for p in range(-5, 13):
        v[p + 6] = smooth(v2, -7, range(-4, 12), p, slab)
    for p in range(-6, 14):
        v1[p + 6] = smooth(v, -6, range(-5, 13), p, slab)
    for q in range(-4, 8):
        put_src1(q + 4, inside(q, 4) * residual_mean(q, range(-6, 14), slab))
    send_second(level2_parts(range(-4, 8), range(-3, 5)))
    send(f.at[pl.ds(7, 7)], f.at[pl.ds(15, 7)], f_send.at[0], f_recv.at[0], at_slab(below))
    send(f.at[pl.ds(8, 7)], f.at[pl.ds(0, 7)], f_send.at[1], f_recv.at[1], at_slab(above))

    gathered(0).wait_recv()
    first = solve_level2(first_source())
    for y in range(12):
        e2[24 * y + 8 : 24 * y + 16, :] = first[y]
    answer = response(first)
    gathered(1).wait_recv()
    second = solve_level2([a + b for a, b in zip(answer, second_source())])
    for y in range(12):
        e2[24 * 16 + 24 * y + 8 : 24 * 16 + 24 * y + 16, :] = second[y]
    spread_level2(0, range(-3, 5))
    spread_level2(1, range(-1, 3))

    for i in range(4):
        pending[i].wait_recv()
    under = [low * plane for i in range(3) for plane in unpacked(f1_in[i])]
    over = [high * plane for i in range(3, 6) for plane in unpacked(f1_in[i])]
    under2 = [low2 * plane for plane in unpacked(f1_in[6])]
    over2 = [high2 * plane for plane in unpacked(f1_in[7])]
    mixed = {q: [part] for q, part in parts.items()}
    for first_plane, planes in ((-5, under), (3, over), (-5, under2), (7, over2)):
        for i, plane in enumerate(planes):
            mixed.setdefault(first_plane + i, []).append(plane)
    for q in range(-5, 9):
        f1[q + 5] = total(mixed[q])
    correct_level1(0, 4)
    pending[4].wait_recv()
    pending[5].wait_recv()
    wide = range(-7, 15)
    for p in wide:
        v2[p + 7] = (PULL[0] * inside(p, 8)) * f[p + 7] + pe1[p // 2 + 4]
    for p in range(-6, 14):
        v[p + 6] = smooth(v2, -7, wide, p, wide)

    for p in range(-5, 13):
        v1[p + 6] = smooth(v, -6, range(-6, 14), p, wide)
    for q in range(-2, 6):
        f1[q + 5] = inside(q, 4) * residual_mean(q, range(-5, 13), wide)
    correct_level1(1, 1)
    for p in range(-1, 9):
        v2[p + 7] = v1[p + 6] + pe1[p // 2 + 4]

    occ_copy.wait_recv()
    mine_occ, left_occ = -occ_out[0:1, :], -occ_in[0:1, :]
    for h in range(4):
        for p in range(2 * h, 2 * h + 2):
            potential = smooth(v2, -7, range(-1, 9), p, slab)
            ret_out[p] = (potential * mine_occ) * own[p]
            v[p] = (potential * left_occ) * left[p]
        planes = pl.ds(2 * h, 2)
        send(ret_out.at[planes], ret_in.at[planes], ret_send.at[h], ret_recv.at[h], at_orb(prev_orb))
    for h in range(4):
        pending[6 + h].wait_recv()
        for p in range(2 * h, 2 * h + 2):
            out_ref[0, p] = v[p] + ret_in[p]

    for copy in halves:
        copy.wait_send()
    occ_copy.wait_send()
    for copy in pending:
        copy.wait_send()
    for g in range(2):
        gathered(g).wait_send()


def on_device(n_orb, n_slab, orbitals, occupations):
    vmem, dma = pltpu.VMEM, pltpu.SemaphoreType.DMA
    f32 = jnp.float32

    def fine(planes):
        return vmem((planes, NY, NX), f32)

    return pl.pallas_call(
        functools.partial(kernel, n_orb, n_slab),
        out_shape=jax.ShapeDtypeStruct(orbitals.shape, f32),
        in_specs=[pl.BlockSpec(memory_space=pltpu.SMEM), pl.BlockSpec(memory_space=pltpu.VMEM)],
        out_specs=pl.BlockSpec(memory_space=pltpu.VMEM),
        scratch_shapes=[
            fine(8), vmem((8, 128), f32), vmem((8, 128), f32),
            fine(22), fine(22), fine(20), fine(20), fine(12),
            vmem((14, 24, 128), f32), vmem((12, ROWS1, 128), f32), vmem((2, 8, 32, 128), f32),
            vmem((3, 24, 128), f32), vmem((8, 24, 128), f32), vmem((MSG2, 128), f32),
            vmem((18 * MSG, 128), f32), vmem((20 * MSG2, 128), f32), vmem((2 * 24 * 16, 128), f32),
            fine(8), fine(8),
            dma((2,)), dma((2,)), dma((2,)), dma((2,)), dma((2,)), dma((4,)), dma((4,)), dma((2,)), dma((2,)), dma((4,)), dma((4,)),
        ],
        compiler_params=pltpu.CompilerParams(collective_id=0, has_side_effects=True, vmem_limit_bytes=32 * 2**20),
    )(occupations, orbitals)


def solution(mesh):
    return jax.shard_map(
        functools.partial(on_device, mesh.shape["orb"], mesh.shape["slab"]),
        mesh=mesh,
        in_specs=(P("orb", "slab", None, None), P("orb")),
        out_specs=P("orb", "slab", None, None),
        check_vma=False,
    )
```

```python
import functools

import jax
import jax.numpy as jnp
import numpy as np
from jax import lax
from jax.experimental import pallas as pl
from jax.experimental.pallas import tpu as pltpu
from jax.sharding import PartitionSpec as P

MESH = pl.DeviceIdType.MESH

NZ, NY, NX = 128, 48, 128
SWEEPS = 6
screening = 0.001
relaxation = 0.8

STEP = [0.25**level for level in range(4)]
CENTRE = [6.0 * step + screening for step in STEP]
KEEP = 1.0 - relaxation
PULL = [relaxation / centre for centre in CENTRE]
SIDE = [pull * step for pull, step in zip(PULL, STEP)]

ROWS1 = 48
FINE = 64
MSG = 16
MSG2 = 24


def response_weights():
    def sides(u):
        padded = np.pad(u, ((0, 0), (1, 1), (0, 0), (0, 0)))
        return padded[:, 2:] + padded[:, :-2] + sum(np.roll(u, by, axis) for by in (1, -1) for axis in (2, 3))

    def smoothed(u, level):
        return KEEP * u + SIDE[level] * sides(u)

    def mean(u):
        b, z, y, x = u.shape
        return u.reshape(b, z // 2, 2, y // 2, 2, x // 2, 2).mean((2, 4, 6))

    def spread(u):
        return u.repeat(2, 1).repeat(2, 2).repeat(2, 3)

    unit = np.zeros((8, 8, 6, 6))
    for z in range(8):
        unit[z, z, 0, 0] = 1.0
    u = spread(smoothed(spread(unit), 1))
    u = smoothed(smoothed(u, 0), 0)
    u = mean(STEP[0] * sides(u) - CENTRE[0] * u)
    u = mean(smoothed(u, 1))
    weights = np.zeros((8, 5, 3, 3))
    for z in range(8):
        for dz in range(-2, 3):
            if 0 <= z + dz < 8:
                weights[z, dz + 2] = u[z, z + dz, :3, :3]
    return weights


def turn(value, by, axis):
    return pltpu.roll(value, by % value.shape[axis], axis)


def put(ref, slot, value):
    ref[slot, 8:56, :] = value
    ref[slot, 7:8, :] = value[47:48]
    ref[slot, 56:57, :] = value[0:1]


def lanes(rows):
    return lax.broadcasted_iota(jnp.int32, (rows, 128), 1)


def in_plane(value, lane_step):
    return (turn(value, 1, 0) + turn(value, -1, 0)) + (turn(value, lane_step, 1) + turn(value, -lane_step, 1))


def swapped(value, bit):
    first = (lanes(value.shape[0]) & bit) == 0
    return jnp.where(first, turn(value, -bit, 1), turn(value, bit, 1))


def total(parts):
    parts = [part for part in parts if part is not None]
    while len(parts) > 1:
        parts = [a + b for a, b in zip(parts[::2], parts[1::2])] + parts[len(parts) // 2 * 2 :]
    return parts[0] if parts else None


def kernel(
    n_orb, n_slab,
    occ_ref, orb_ref, out_ref,
    own, left, occ_out, occ_in, f, v2, v, v1, pe1, f1, src1, pe2, e1, f1_out, f1_in, f2_out, f2_in, msg2, gather, gather2, e2, e2b,
    ret_out, ret_in, mine_out,
    local_sem, orb_send, orb_recv, occ_sems, gat_send, gat_recv, f1_send, f1_recv, f_send, f_recv, ret_send, ret_recv,
):
    o, s = lax.axis_index("orb"), lax.axis_index("slab")
    prev_orb, next_orb = lax.rem(o + n_orb - 1, n_orb), lax.rem(o + 1, n_orb)
    above, below = lax.rem(s + 1, n_slab), lax.rem(s + n_slab - 1, n_slab)
    odd = lax.rem(s, 2)

    def at_slab(index):
        return {"slab": index}

    def at_orb(index):
        return {"orb": index}

    mine = pltpu.make_async_copy(orb_ref.at[0], own, local_sem)
    mine.start()
    peers = sorted(((x, y) for x in range(4) for y in range(4) if x or y), key=lambda d: -min(d[0], 4 - d[0]) - min(d[1], 4 - d[1]))
    peers = [4 * lax.rem(s // 4 + y, 4) + lax.rem(s + x, 4) for x, y in peers]

    barrier = pltpu.get_barrier_semaphore()
    pl.semaphore_signal(barrier, inc=1, device_id=at_orb(next_orb), device_id_type=MESH)
    pl.semaphore_signal(barrier, inc=1, device_id=at_orb(prev_orb), device_id_type=MESH)
    for peer in peers:
        pl.semaphore_signal(barrier, inc=1, device_id=at_slab(peer), device_id_type=MESH)

    occ_out[...] = jnp.full((8, 128), occ_ref[0], jnp.float32)
    for slot in (0, 17):
        gather[pl.ds(slot * MSG, MSG), :] = jnp.zeros((MSG, 128), jnp.float32)
    for slot in (0, 18):
        gather2[pl.ds(slot * MSG2, 2 * MSG2), :] = jnp.zeros((2 * MSG2, 128), jnp.float32)
    e2[...] = jnp.zeros_like(e2)
    e2b[...] = jnp.zeros_like(e2b)
    src1[...] = jnp.zeros_like(src1)
    low = jnp.where(s > 0, 1.0, 0.0).astype(jnp.float32)
    high = jnp.where(s < n_slab - 1, 1.0, 0.0).astype(jnp.float32)
    low2 = jnp.where(s > 1, 1.0, 0.0).astype(jnp.float32)
    high2 = jnp.where(s < n_slab - 2, 1.0, 0.0).astype(jnp.float32)

    def inside(plane, count):
        return low if plane < 0 else high if plane >= count else 1.0

    mine.wait()
    pl.semaphore_wait(barrier, n_slab + 1)

    halves = []
    for h in range(2):
        planes = pl.ds(4 * h, 4)
        halves.append(pltpu.make_async_remote_copy(
            own.at[planes], left.at[planes], orb_send.at[h], orb_recv.at[h],
            device_id=at_orb(next_orb), device_id_type=MESH))
        halves[-1].start()
    occ_copy = pltpu.make_async_remote_copy(
        occ_out, occ_in, occ_sems.at[0], occ_sems.at[1], device_id=at_orb(next_orb), device_id_type=MESH)
    occ_copy.start()

    for h in range(2):
        halves[h].wait_recv()
        for p in range(4 * h, 4 * h + 4):
            put(f, 3 + p, own[p] * left[p])

    def remote(src, dst, send_sem, recv_sem, device):
        return pltpu.make_async_remote_copy(src, dst, send_sem, recv_sem, device_id=device, device_id_type=MESH)

    pending = []

    def send(src, dst, send_sem, recv_sem, device):
        copy = remote(src, dst, send_sem, recv_sem, device)
        copy.start()
        pending.append(copy)
        return copy

    def restricted(pair, beyond, source, centre, side, bit):
        beyond = total([part for plane in beyond for part in plane[:2]])
        terms = []
        if pair:
            even, odd_, before, after = [total([plane[i] for plane in pair]) for i in range(4)]
            both = even + odd_
            terms.append(centre * both)
            around = total([both + both, before, after, turn(both, bit, 1), turn(both, -bit, 1), beyond])
        else:
            around = beyond
        terms.append(side * around)
        terms += [part for plane in source for part in plane]
        mean = total(terms)
        return 0.125 * (mean + swapped(mean, bit))

    def fine_rows(ref, plane):
        return [ref[plane, pl.ds(8 + start, 24, stride=2), :] for start in (0, 1, -1, 2)]

    def put_src1(slot, value):
        src1[slot, 8:32, :] = value
        src1[slot, 7:8, :] = value[23:24]
        src1[slot, 32:33, :] = value[0:1]

    def coarse_rows(slot):
        return [src1[slot, pl.ds(8 + start, MSG, stride=2), :] for start in (0, 1, -1, 2)]

    lane16 = lanes(MSG)
    place16 = (lane16 + 2 * odd) & 3

    def level2_parts(have, planes):
        parts = {}
        for d in planes:
            pair = [coarse_rows(q + 4) for q in (2 * d, 2 * d + 1) if q in have]
            beyond = [coarse_rows(q + 4) for q in (2 * d - 1, 2 * d + 2) if q in have]
            parts[d] = restricted(pair, beyond, [], KEEP, SIDE[1], 2)
        return parts

    def laid(parts, planes):
        by_place = {d % 4: parts[d] for d in planes}
        return jnp.where(place16 < 2, jnp.where(place16 == 0, by_place[0], by_place[1]), jnp.where(place16 == 2, by_place[2], by_place[3]))

    slot1 = pl.ds(pl.multiple_of((s + 1) * MSG, MSG), MSG)
    slot2 = pl.ds(pl.multiple_of((s + 2) * MSG2, MSG2), MSG2)

    def send_first(parts):
        gather[slot1, :] = laid(parts, range(-1, 3))
        for peer in peers:
            remote(gather.at[slot1], gather.at[slot1], gat_send.at[0], gat_recv.at[0], at_slab(peer)).start()

    def send_second(parts):
        msg2[0:12, :] = laid(parts, range(-1, 3))[0:12]
        msg2[12:24, :] = laid(parts, (-3, -2, 3, 4))[0:12]
        gather2[slot2, :] = msg2[...]
        for peer in peers:
            remote(msg2, gather2.at[slot2], gat_send.at[1], gat_recv.at[1], at_slab(peer)).start()

    def gathered(g):
        most = gather.at[pl.ds(0, (n_slab - 1) * MSG)] if g == 0 else gather2.at[pl.ds(0, (n_slab - 1) * MSG2)]
        return remote(most, most, gat_send.at[g], gat_recv.at[g], at_slab(above))

    row8 = lax.broadcasted_iota(jnp.int32, (8, 128), 0)
    lane8 = lanes(8)
    first_row, last_row = row8 == 0, row8 == 7

    def level2_sides(u):
        result = []
        for y in range(12):
            here = u[y]
            up = jnp.where(last_row, 0.0, turn(turn(here, 3, 1), -1, 0))
            down = jnp.where(first_row, 0.0, turn(turn(here, -3, 1), 1, 0))
            up = jnp.where((lane8 & 3) == 3, up, turn(here, -1, 1))
            down = jnp.where((lane8 & 3) == 0, down, turn(here, 1, 1))
            x = turn(here, 4, 1) + turn(here, -4, 1)
            result.append(total([u[(y + 1) % 12], u[(y + 11) % 12], up, down, x]))
        return result

    def level3_sides(u):
        result = []
        lower = (lane8 & 2) == 0
        for y in range(6):
            here = u[y]
            a, b = turn(here, -2, 1), turn(here, 2, 1)
            far = jnp.where(lower, jnp.where(first_row, 0.0, turn(a, 1, 0)), jnp.where(last_row, 0.0, turn(b, -1, 0)))
            x = turn(here, 8, 1) + turn(here, -8, 1)
            result.append(total([u[(y + 1) % 6], u[(y + 5) % 6], jnp.where(lower, a, b), far, x]))
        return result

    place8 = lane8 & 3

    def first_source():
        source = []
        for y in range(12):
            even, odd_, even_after, odd_before = [gather[pl.ds(MSG * k + y, 8, stride=2 * MSG), :] for k in (1, 2, 3, 0)]
            source.append(jnp.where(place8 == 3, even_after, even) + jnp.where(place8 == 0, odd_before, odd_))
        return source

    def second_source():
        source = []
        for y in range(12):
            even, odd_, even_after, odd_before = [gather2[pl.ds(MSG2 * k + y, 8, stride=2 * MSG2), :] for k in (2, 3, 4, 1)]
            near = jnp.where(place8 == 3, even_after, even) + jnp.where(place8 == 0, odd_before, odd_)
            even_before, even, even_after, odd_before, odd_, odd_after = [
                gather2[pl.ds(MSG2 * k + 12 + y, 8, stride=2 * MSG2), :] for k in (0, 2, 4, 1, 3, 5)]
            far = jnp.where(place8 == 0, even_before, jnp.where(place8 == 3, even, even_after))
            far = far + jnp.where(place8 == 0, odd_, jnp.where(place8 == 3, odd_after, odd_before))
            source.append(near + far)
        return source

    def response(u):
        weights = response_weights()
        plane = 4 * row8 + place8

        def weight(dz, dy, dx):
            inner = float(weights[4, dz + 2, dy, dx])
            value = inner
            for at, z in ((0, 0), (1, 1), (30, 6), (31, 7)):
                if abs(weights[z, dz + 2, dy, dx] - inner) > 1e-12:
                    value = jnp.where(plane == at, jnp.float32(weights[z, dz + 2, dy, dx]), value)
            return value

        x1 = [turn(a, 4, 1) + turn(a, -4, 1) for a in u]
        x2 = [turn(a, 8, 1) + turn(a, -8, 1) for a in u]

        def beside(a, y, by):
            return a[(y + by) % 12] + a[(y - by) % 12]

        groups = ((0, 0), (0, 1), (0, 2), (1, 1), (1, 2))
        by_dz = {dz: [weight(dz, *group) for group in groups] for dz in (-1, 0, 1)}
        two = [float(weights[4, 4, dy, dx]) for dy, dx in ((0, 0), (0, 1), (1, 1))]
        result = []
        for y in range(12):
            sums = [u[y], x1[y] + beside(u, y, 1), x2[y] + beside(u, y, 2), beside(x1, y, 1), beside(x2, y, 1) + beside(x1, y, 2)]
            here, up, down = [total([w * a for w, a in zip(by_dz[dz], sums)]) for dz in (0, -1, 1)]
            far = two[0] * sums[0] + two[1] * sums[1] + two[2] * sums[3]
            up = jnp.where(place8 == 3, jnp.where(last_row, 0.0, turn(turn(up, 3, 1), -1, 0)), turn(up, -1, 1))
            down = jnp.where(place8 == 0, jnp.where(first_row, 0.0, turn(turn(down, -3, 1), 1, 0)), turn(down, 1, 1))
            a, b = turn(far, 2, 1), turn(far, -2, 1)
            far = jnp.where(place8 >= 2, a + jnp.where(last_row, 0.0, turn(a, -1, 0)), b + jnp.where(first_row, 0.0, turn(b, 1, 0)))
            result.append(total([here, up, down, far]))
        return result

    def solve_level2(source):
        sides = level2_sides(source)
        residual = [KEEP * a + SIDE[2] * b for a, b in zip(source, sides)]
        source3 = []
        for y in range(6):
            pair = residual[2 * y] + residual[2 * y + 1]
            pair = pair + swapped(pair, 1)
            source3.append(0.125 * (pair + swapped(pair, 4)))
        pull = [PULL[3] * a for a in source3]
        iterate = pull
        for _ in range(SWEEPS - 1):
            sides = level3_sides(iterate)
            iterate = [KEEP * a + b + SIDE[3] * c for a, b, c in zip(iterate, pull, sides)]
        pull = [PULL[2] * a for a in source]
        u = [a + iterate[y // 2] for y, a in enumerate(pull)]
        sides = level2_sides(u)
        return [KEEP * a + b + SIDE[2] * c for a, b, c in zip(u, pull, sides)]

    def spread_level2(g, ds):
        row = 8 + s // 2
        a, b, c = [(e2, e2b)[g][pl.ds(row + by, MSG, stride=24), :] for by in (-1, 0, 1)]
        for d in ds:
            rows = a if d == -3 else jnp.where(odd == 1, b, a) if d < 0 else b if d < 2 else jnp.where(odd == 1, c, b) if d < 4 else c
            value = jnp.where(place16 == d % 4, rows, 0.0)
            value = value + swapped(value, 1)
            value = value + swapped(value, 2)
            pe2[g, d + 3, pl.ds(0, MSG, stride=2), :] = value
            pe2[g, d + 3, pl.ds(1, MSG, stride=2), :] = value

    even24 = (lanes(24) & 1) == 0

    def packed(a, b):
        return jnp.where(even24, a, b)

    def unpacked(value):
        return jnp.where(even24, value, turn(value, 1, 1)), jnp.where(even24, turn(value, -1, 1), value)

    def put_pe1(q, value):
        pe1[q + 4, pl.ds(8, 24, stride=2), :] = value
        pe1[q + 4, pl.ds(9, 24, stride=2), :] = value
        pe1[q + 4, 7:8, :] = value[23:24]
        pe1[q + 4, 56:57, :] = value[0:1]

    def correct_level1(g, reach):
        u = {q: pe2[g, q // 2 + 3, 0:24, :] for q in range(-reach - 1, 5 + reach)}
        return {
            q: KEEP * u[q] + (SIDE[1] * inside(q, 4)) * total([u[q - 1], u[q + 1], in_plane(u[q], 2)])
            for q in range(-reach, 4 + reach)
        }

    def base_level1(planes):
        answer = {}
        for q in planes:
            here = PULL[1] * f1[q + 3]
            sides = total([PULL[1] * f1[q + 2], PULL[1] * f1[q + 4], in_plane(here, 2)])
            answer[q] = (KEEP + 1.0) * here + (SIDE[1] * inside(q, 4)) * sides
        return answer

    def smooth(at, planes, plane, source):
        flag = inside(plane, 8)
        near = [at(p)[0] for p in (plane - 1, plane + 1) if p in planes]
        terms = []
        if plane in planes:
            here, before, after = at(plane)
            near += [before, after, turn(here, 1, 1) + turn(here, -1, 1)]
            terms.append(KEEP * here)
        if plane in source:
            terms.append((PULL[0] * flag) * f[plane + 3, 8:56, :])
        return total(terms + [(SIDE[0] * flag) * total(near)])

    def rows_at(ref, slot):
        return ref[slot, 8:56, :], ref[slot, 7:55, :], ref[slot, 9:57, :]

    def at_v2(p):
        return rows_at(v2, p + 4)

    def at_v(p):
        return rows_at(v, p + 6)

    def at_coarse(p):
        return rows_at(pe1, p // 2 + 4)

    def residual_mean(q, planes, source):
        pair = [fine_rows(v1, p + 6) for p in (2 * q, 2 * q + 1) if p in planes]
        beyond = [fine_rows(v1, p + 6) for p in (2 * q - 1, 2 * q + 2) if p in planes]
        rows = [fine_rows(f, p + 3)[:2] for p in (2 * q, 2 * q + 1) if p in source]
        return restricted(pair, beyond, rows, -CENTRE[0], STEP[0], 1)

    slab = range(8)
    for q in range(-1, 5):
        pair = [fine_rows(f, p + 3) for p in (2 * q, 2 * q + 1) if p in slab]
        beyond = [fine_rows(f, p + 3) for p in (2 * q - 1, 2 * q + 2) if p in slab]
        put_src1(q + 4, restricted(pair, beyond, [], KEEP, SIDE[0] * inside(q, 4), 1))
    send_first(level2_parts(range(-1, 5), range(-1, 3)))
    parts = {q: src1[q + 4, 8:32, :] for q in range(-1, 5)}
    for i in range(3):
        f1_out[i] = packed(parts[2 * i - 1], parts[2 * i])
    below2, above2 = lax.rem(s + n_slab - 2, n_slab), lax.rem(s + 2, n_slab)
    send(f1_out.at[pl.ds(0, 2)], f1_in.at[pl.ds(2, 2)], f1_send.at[0], f1_recv.at[0], at_slab(below))
    send(f1_out.at[pl.ds(1, 2)], f1_in.at[pl.ds(0, 2)], f1_send.at[1], f1_recv.at[1], at_slab(above))

    pulled = {q: PULL[1] * parts[q] for q in parts}
    for q in range(-2, 6):
        near = [pulled.get(q - 1), pulled.get(q + 1)]
        terms = []
        if q in parts:
            near.append(in_plane(pulled[q], 2))
            terms = [(KEEP + 1.0) * pulled[q]]
        put_pe1(q, total(terms + [(SIDE[1] * inside(q, 4)) * total(near)]))
    for p in range(-4, 12):
        put(v2, p + 4, PULL[0] * f[p + 3, 8:56, :] + at_coarse(p)[0] if p in slab else at_coarse(p)[0])
    for p in range(-5, 13):
        put(v, p + 6, smooth(at_v2, range(-4, 12), p, slab))
    for p in range(-6, 14):
        put(v1, p + 6, smooth(at_v, range(-5, 13), p, slab))
    for q in range(-4, 8):
        put_src1(q + 4, inside(q, 4) * residual_mean(q, range(-6, 14), slab))
    send_second(level2_parts(range(-4, 8), range(-3, 5)))
    shares = {q: src1[q + 4, 8:32, :] for q in (-4, -3, -2, -1, 2, 3, 0, 1, 4, 5, 6, 7)}
    for i, q in enumerate((-4, 0, 2, 6)):
        f2_out[i] = packed(shares[q], shares[q + 1])
    for i, device in enumerate((below2, below, above, above2)):
        send(f2_out.at[i], f2_in.at[i], f1_send.at[2 + i], f1_recv.at[2 + i], at_slab(device))
    send(f.at[pl.ds(3, 3), pl.ds(8, NY)], f.at[pl.ds(11, 3), pl.ds(8, NY)], f_send.at[0], f_recv.at[0], at_slab(below))
    send(f.at[pl.ds(8, 3), pl.ds(8, NY)], f.at[pl.ds(0, 3), pl.ds(8, NY)], f_send.at[1], f_recv.at[1], at_slab(above))

    pending[0].wait_recv()
    pending[1].wait_recv()
    under = [low * plane for i in range(2) for plane in unpacked(f1_in[i])]
    over = [high * plane for i in range(2, 4) for plane in unpacked(f1_in[i])]
    mixed = {q: [part] for q, part in parts.items()}
    for first_plane, planes in ((-3, under), (3, over)):
        for i, plane in enumerate(planes):
            mixed.setdefault(first_plane + i, []).append(plane)
    for q in range(-3, 7):
        f1[q + 3] = total(mixed[q])
    base = base_level1(range(-2, 6))
    for q in base:
        e1[q + 2] = base[q]

    gathered(0).wait_recv()
    first = solve_level2(first_source())
    for y in range(12):
        e2[24 * y + 8 : 24 * y + 16, :] = first[y]
    answer = response(first)

    spread_level2(0, range(-3, 5))
    answer1 = correct_level1(0, 4)
    for q in answer1:
        put_pe1(q, answer1[q])
    for lowest in (-6, 6):
        for p in range(lowest, lowest + 8):
            put(v, p + 6, smooth(at_coarse, range(-8, 16), p, ()))
        for p in range(lowest + 1, lowest + 7):
            put(v1, p + 6, smooth(at_v, range(lowest, lowest + 8), p, ()))
    for i in (2, 3, 4, 5, 6, 7):
        pending[i].wait_recv()
    gathered(1).wait_recv()
    second = solve_level2([a + b for a, b in zip(answer, second_source())])
    for y in range(12):
        e2b[24 * y + 8 : 24 * y + 16, :] = second[y]
    beside = {}
    for q, near, far, near_flag, far_flag in ((-2, 2, 3, low, low2), (4, 1, 0, high, high2)):
        for i, (a, b) in enumerate(zip(unpacked(f2_in[near]), unpacked(f2_in[far]))):
            own_part = inside(q, 4) * residual_mean(q + i, range(-6, 14), ())
            beside[q + i] = total([shares[q + i], own_part, near_flag * a, far_flag * b])
    for q in range(-2, 6):
        put_pe1(q, answer1[q] + e1[q + 2])
    for p in range(-3, 11):
        put(v2, p + 4, (PULL[0] * inside(p, 8)) * f[p + 3, 8:56, :] + at_coarse(p)[0])
    for p in range(-2, 10):
        put(v, p + 6, smooth(at_v2, range(-3, 11), p, range(-3, 11)))

    for p in range(-1, 9):
        put(v1, p + 6, smooth(at_v, range(-2, 10), p, range(-3, 11)))
    for q in range(-2, 6):
        f1[q + 3] = residual_mean(q, range(-1, 9), slab) if q in range(4) else beside[q]
    spread_level2(1, range(-1, 3))
    answer1 = correct_level1(1, 1)
    base = base_level1(range(-1, 5))
    for q in answer1:
        put_pe1(q, answer1[q] + base[q])
    for p in range(-1, 9):
        put(v2, p + 4, v1[p + 6, 8:56, :] + at_coarse(p)[0])

    occ_copy.wait_recv()
    mine_occ, left_occ = -occ_out[0:1, :], -occ_in[0:1, :]
    for h in range(4):
        for p in range(2 * h, 2 * h + 2):
            potential = smooth(at_v2, range(-1, 9), p, slab)
            ret_out[p] = (potential * mine_occ) * own[p]
            mine_out[p] = (potential * left_occ) * left[p]
        planes = pl.ds(2 * h, 2)
        send(ret_out.at[planes], ret_in.at[planes], ret_send.at[h], ret_recv.at[h], at_orb(prev_orb))
    for h in range(4):
        pending[8 + h].wait_recv()
        for p in range(2 * h, 2 * h + 2):
            out_ref[0, p] = mine_out[p] + ret_in[p]

    for copy in halves:
        copy.wait_send()
    occ_copy.wait_send()
    for copy in pending:
        copy.wait_send()
    for g in range(2):
        gathered(g).wait_send()


def on_device(n_orb, n_slab, orbitals, occupations):
    vmem, dma = pltpu.VMEM, pltpu.SemaphoreType.DMA
    f32 = jnp.float32

    def fine(planes):
        return vmem((planes, NY, NX), f32)

    def tall(planes):
        return vmem((planes, FINE, NX), f32)

    return pl.pallas_call(
        functools.partial(kernel, n_orb, n_slab),
        out_shape=jax.ShapeDtypeStruct(orbitals.shape, f32),
        in_specs=[pl.BlockSpec(memory_space=pltpu.SMEM), pl.BlockSpec(memory_space=pltpu.HBM)],
        out_specs=pl.BlockSpec(memory_space=pltpu.VMEM),
        scratch_shapes=[
            fine(8), fine(8), vmem((8, 128), f32), vmem((8, 128), f32),
            tall(14), tall(16), tall(20), tall(20), tall(12),
            vmem((10, 24, 128), f32), vmem((12, ROWS1, 128), f32), vmem((2, 8, 32, 128), f32), vmem((8, 24, 128), f32),
            vmem((3, 24, 128), f32), vmem((4, 24, 128), f32), vmem((4, 24, 128), f32), vmem((4, 24, 128), f32), vmem((MSG2, 128), f32),
            vmem((18 * MSG, 128), f32), vmem((20 * MSG2, 128), f32), vmem((24 * 16, 128), f32), vmem((24 * 16, 128), f32),
            fine(8), fine(8), fine(8),
            dma, dma((2,)), dma((2,)), dma((2,)), dma((2,)), dma((2,)), dma((6,)), dma((6,)), dma((2,)), dma((2,)), dma((4,)), dma((4,)),
        ],
        compiler_params=pltpu.CompilerParams(collective_id=0, has_side_effects=True, vmem_limit_bytes=32 * 2**20),
    )(occupations, pltpu.with_memory_space_constraint(orbitals, pltpu.HBM))


def solution(mesh):
    return jax.shard_map(
        functools.partial(on_device, mesh.shape["orb"], mesh.shape["slab"]),
        mesh=mesh,
        in_specs=(P("orb", "slab", None, None), P("orb")),
        out_specs=P("orb", "slab", None, None),
        check_vma=False,
    )
```

```python
import functools

import jax
import jax.numpy as jnp
import numpy as np
from jax import lax
from jax.experimental import pallas as pl
from jax.experimental.pallas import tpu as pltpu
from jax.sharding import PartitionSpec as P

MESH = pl.DeviceIdType.MESH

NZ, NY, NX = 128, 48, 128
SWEEPS = 6
screening = 0.001
relaxation = 0.8

STEP = [0.25**level for level in range(4)]
CENTRE = [6.0 * step + screening for step in STEP]
KEEP = 1.0 - relaxation
PULL = [relaxation / centre for centre in CENTRE]
SIDE = [pull * step for pull, step in zip(PULL, STEP)]

ROWS1 = 48
FINE = 64
MSG = 16
MSG2 = 24


def response_weights():
    def sides(u):
        padded = np.pad(u, ((0, 0), (1, 1), (0, 0), (0, 0)))
        return padded[:, 2:] + padded[:, :-2] + sum(np.roll(u, by, axis) for by in (1, -1) for axis in (2, 3))

    def smoothed(u, level):
        return KEEP * u + SIDE[level] * sides(u)

    def mean(u):
        b, z, y, x = u.shape
        return u.reshape(b, z // 2, 2, y // 2, 2, x // 2, 2).mean((2, 4, 6))

    def spread(u):
        return u.repeat(2, 1).repeat(2, 2).repeat(2, 3)

    unit = np.zeros((8, 8, 6, 6))
    for z in range(8):
        unit[z, z, 0, 0] = 1.0
    u = spread(smoothed(spread(unit), 1))
    u = smoothed(smoothed(u, 0), 0)
    u = mean(STEP[0] * sides(u) - CENTRE[0] * u)
    u = mean(smoothed(u, 1))
    weights = np.zeros((8, 5, 3, 3))
    for z in range(8):
        for dz in range(-2, 3):
            if 0 <= z + dz < 8:
                weights[z, dz + 2] = u[z, z + dz, :3, :3]
    return weights


def turn(value, by, axis):
    return pltpu.roll(value, by % value.shape[axis], axis)


def put(ref, slot, value):
    ref[slot, 8:56, :] = value
    ref[slot, 7:8, :] = value[47:48]
    ref[slot, 56:57, :] = value[0:1]


def lanes(rows):
    return lax.broadcasted_iota(jnp.int32, (rows, 128), 1)


def in_plane(value, lane_step):
    return (turn(value, 1, 0) + turn(value, -1, 0)) + (turn(value, lane_step, 1) + turn(value, -lane_step, 1))


def swapped(value, bit):
    first = (lanes(value.shape[0]) & bit) == 0
    return jnp.where(first, turn(value, -bit, 1), turn(value, bit, 1))


def total(parts):
    parts = [part for part in parts if part is not None]
    while len(parts) > 1:
        parts = [a + b for a, b in zip(parts[::2], parts[1::2])] + parts[len(parts) // 2 * 2 :]
    return parts[0] if parts else None


def kernel(
    n_orb, n_slab,
    occ_ref, orb_ref, out_ref,
    own, orb_x, orb_y, occ_own, occ_x, occ_y, f, v2, v, v1, pe1, f1, src1, pe2, e1, f1_out, f1_in, f2_out, f2_in, msg2, gather, gather2, e2, e2b,
    out_y, in_y, both_x, orb_n, occ_n, last, fix_out, fix_in,
    go, local_sem, orb_send, orb_recv, next_send, next_recv, gat_send, gat_recv, f1_send, f1_recv, f_send, f_recv, ret_send, ret_recv, prev_send, prev_recv, before_send, before_recv,
):
    o, s = lax.axis_index("orb"), lax.axis_index("slab")
    core = lax.rem(o, 2)
    partner = {"orb": o + 1 - 2 * core}
    after, before = {"orb": lax.rem(o + 2, n_orb)}, {"orb": lax.rem(o + n_orb - 2, n_orb)}
    above, below = lax.rem(s + 1, n_slab), lax.rem(s + n_slab - 1, n_slab)
    odd = lax.rem(s, 2)

    def at_slab(index):
        return {"slab": index}

    mine = pltpu.make_async_copy(orb_ref.at[0], own, local_sem)
    mine.start()
    peers = sorted(((x, y) for x in range(4) for y in range(4) if x or y), key=lambda d: -min(d[0], 4 - d[0]) - min(d[1], 4 - d[1]))
    peers = [4 * lax.rem(s // 4 + y, 4) + lax.rem(s + x, 4) for x, y in peers]

    barrier = pltpu.get_barrier_semaphore()

    def greet(device):
        pl.semaphore_signal(barrier, inc=1, device_id=device, device_id_type=MESH)

    greet(partner)

    @pl.when(core == 0)
    def _():
        for peer in peers:
            greet({"orb": o, "slab": peer})

    @pl.when(core == 1)
    def _():
        greet(before)
        greet({"orb": lax.rem(o + 1, n_orb)})
        for peer in peers:
            greet({"orb": o - 1, "slab": peer})

    occ_own[...] = jnp.full((8, 128), occ_ref[0], jnp.float32)
    for slot in (0, 17):
        gather[pl.ds(slot * MSG, MSG), :] = jnp.zeros((MSG, 128), jnp.float32)
    for slot in (0, 18):
        gather2[pl.ds(slot * MSG2, 2 * MSG2), :] = jnp.zeros((2 * MSG2, 128), jnp.float32)
    e2[...] = jnp.zeros_like(e2)
    e2b[...] = jnp.zeros_like(e2b)
    src1[...] = jnp.zeros_like(src1)
    low = jnp.where(s > 0, 1.0, 0.0).astype(jnp.float32)
    high = jnp.where(s < n_slab - 1, 1.0, 0.0).astype(jnp.float32)
    low2 = jnp.where(s > 1, 1.0, 0.0).astype(jnp.float32)
    high2 = jnp.where(s < n_slab - 2, 1.0, 0.0).astype(jnp.float32)

    def inside(plane, count):
        return low if plane < 0 else high if plane >= count else 1.0

    def remote(src, dst, send_sem, recv_sem, device):
        return pltpu.make_async_remote_copy(src, dst, send_sem, recv_sem, device_id=device, device_id_type=MESH)

    mine.wait()

    @pl.when(core == 0)
    def _():
        pl.semaphore_wait(barrier, 2 * n_slab)
        pl.semaphore_signal(go, inc=1, device_id=partner, device_id_type=MESH)

    @pl.when(core == 1)
    def _():
        pl.semaphore_wait(barrier, 2)

    to_next = [
        remote(own, orb_y, next_send.at[0], next_recv.at[0], after),
        remote(occ_own, occ_y, next_send.at[1], next_recv.at[1], after),
    ]
    to_partner = [
        remote(own, orb_x, orb_send.at[0], orb_recv.at[0], partner),
        remote(occ_own, occ_x, orb_send.at[1], orb_recv.at[1], partner),
    ]

    @pl.when(core == 1)
    def _():
        for copy in to_next:
            copy.start()

    for copy in to_partner:
        copy.start()

    @pl.when(core == 0)
    def _():
        occ_y[...] = occ_own[...]
        orb_y[...] = own[...]

    to_partner[0].wait_recv()

    @pl.when(core == 1)
    def _():
        to_next[0].wait_recv()

    for p in range(8):
        put(f, 3 + p, orb_x[p] * orb_y[p])
    to_partner[1].wait_recv()

    to_before = [
        remote(orb_x, orb_n, before_send.at[0], before_recv.at[0], before),
        remote(occ_x, occ_n, before_send.at[1], before_recv.at[1], before),
    ]

    pending = []

    def send(src, dst, send_sem, recv_sem, device):
        copy = remote(src, dst, send_sem, recv_sem, device)
        copy.start()
        pending.append(copy)
        return copy

    def restricted(pair, beyond, source, centre, side, bit):
        beyond = total([part for plane in beyond for part in plane[:2]])
        terms = []
        if pair:
            even, odd_, before, after = [total([plane[i] for plane in pair]) for i in range(4)]
            both = even + odd_
            terms.append(centre * both)
            around = total([both + both, before, after, turn(both, bit, 1), turn(both, -bit, 1), beyond])
        else:
            around = beyond
        terms.append(side * around)
        terms += [part for plane in source for part in plane]
        mean = total(terms)
        return 0.125 * (mean + swapped(mean, bit))

    def fine_rows(ref, plane):
        return [ref[plane, pl.ds(8 + start, 24, stride=2), :] for start in (0, 1, -1, 2)]

    def put_src1(slot, value):
        src1[slot, 8:32, :] = value
        src1[slot, 7:8, :] = value[23:24]
        src1[slot, 32:33, :] = value[0:1]

    def coarse_rows(slot):
        return [src1[slot, pl.ds(8 + start, MSG, stride=2), :] for start in (0, 1, -1, 2)]

    lane16 = lanes(MSG)
    place16 = (lane16 + 2 * odd) & 3

    def level2_parts(have, planes):
        parts = {}
        for d in planes:
            pair = [coarse_rows(q + 4) for q in (2 * d, 2 * d + 1) if q in have]
            beyond = [coarse_rows(q + 4) for q in (2 * d - 1, 2 * d + 2) if q in have]
            parts[d] = restricted(pair, beyond, [], KEEP, SIDE[1], 2)
        return parts

    def laid(parts, planes):
        by_place = {d % 4: parts[d] for d in planes}
        return jnp.where(place16 < 2, jnp.where(place16 == 0, by_place[0], by_place[1]), jnp.where(place16 == 2, by_place[2], by_place[3]))

    slot1 = pl.ds(pl.multiple_of((s + 1) * MSG, MSG), MSG)
    slot2 = pl.ds(pl.multiple_of((s + 2) * MSG2, MSG2), MSG2)

    def send_first(parts):
        gather[slot1, :] = laid(parts, range(-1, 3))

        @pl.when(core == 1)
        def _():
            pl.semaphore_wait(go, 1)

        for peer in peers:
            remote(gather.at[slot1], gather.at[slot1], gat_send.at[0], gat_recv.at[0], at_slab(peer)).start()

    def send_second(parts):
        msg2[0:12, :] = laid(parts, range(-1, 3))[0:12]
        msg2[12:24, :] = laid(parts, (-3, -2, 3, 4))[0:12]
        gather2[slot2, :] = msg2[...]
        for peer in peers:
            remote(msg2, gather2.at[slot2], gat_send.at[1], gat_recv.at[1], at_slab(peer)).start()

    def gathered(g):
        most = gather.at[pl.ds(0, (n_slab - 1) * MSG)] if g == 0 else gather2.at[pl.ds(0, (n_slab - 1) * MSG2)]
        return remote(most, most, gat_send.at[g], gat_recv.at[g], at_slab(above))

    row8 = lax.broadcasted_iota(jnp.int32, (8, 128), 0)
    lane8 = lanes(8)
    first_row, last_row = row8 == 0, row8 == 7

    def level2_sides(u):
        result = []
        for y in range(12):
            here = u[y]
            up = jnp.where(last_row, 0.0, turn(turn(here, 3, 1), -1, 0))
            down = jnp.where(first_row, 0.0, turn(turn(here, -3, 1), 1, 0))
            up = jnp.where((lane8 & 3) == 3, up, turn(here, -1, 1))
            down = jnp.where((lane8 & 3) == 0, down, turn(here, 1, 1))
            x = turn(here, 4, 1) + turn(here, -4, 1)
            result.append(total([u[(y + 1) % 12], u[(y + 11) % 12], up, down, x]))
        return result

    def level3_sides(u):
        result = []
        lower = (lane8 & 2) == 0
        for y in range(6):
            here = u[y]
            a, b = turn(here, -2, 1), turn(here, 2, 1)
            far = jnp.where(lower, jnp.where(first_row, 0.0, turn(a, 1, 0)), jnp.where(last_row, 0.0, turn(b, -1, 0)))
            x = turn(here, 8, 1) + turn(here, -8, 1)
            result.append(total([u[(y + 1) % 6], u[(y + 5) % 6], jnp.where(lower, a, b), far, x]))
        return result

    place8 = lane8 & 3

    def first_source():
        source = []
        for y in range(12):
            even, odd_, even_after, odd_before = [gather[pl.ds(MSG * k + y, 8, stride=2 * MSG), :] for k in (1, 2, 3, 0)]
            source.append(jnp.where(place8 == 3, even_after, even) + jnp.where(place8 == 0, odd_before, odd_))
        return source

    def second_source():
        source = []
        for y in range(12):
            even, odd_, even_after, odd_before = [gather2[pl.ds(MSG2 * k + y, 8, stride=2 * MSG2), :] for k in (2, 3, 4, 1)]
            near = jnp.where(place8 == 3, even_after, even) + jnp.where(place8 == 0, odd_before, odd_)
            even_before, even, even_after, odd_before, odd_, odd_after = [
                gather2[pl.ds(MSG2 * k + 12 + y, 8, stride=2 * MSG2), :] for k in (0, 2, 4, 1, 3, 5)]
            far = jnp.where(place8 == 0, even_before, jnp.where(place8 == 3, even, even_after))
            far = far + jnp.where(place8 == 0, odd_, jnp.where(place8 == 3, odd_after, odd_before))
            source.append(near + far)
        return source

    def response(u):
        weights = response_weights()
        plane = 4 * row8 + place8

        def weight(dz, dy, dx):
            inner = float(weights[4, dz + 2, dy, dx])
            value = inner
            for at, z in ((0, 0), (1, 1), (30, 6), (31, 7)):
                if abs(weights[z, dz + 2, dy, dx] - inner) > 1e-12:
                    value = jnp.where(plane == at, jnp.float32(weights[z, dz + 2, dy, dx]), value)
            return value

        x1 = [turn(a, 4, 1) + turn(a, -4, 1) for a in u]
        x2 = [turn(a, 8, 1) + turn(a, -8, 1) for a in u]

        def beside(a, y, by):
            return a[(y + by) % 12] + a[(y - by) % 12]

        groups = ((0, 0), (0, 1), (0, 2), (1, 1), (1, 2))
        by_dz = {dz: [weight(dz, *group) for group in groups] for dz in (-1, 0, 1)}
        two = [float(weights[4, 4, dy, dx]) for dy, dx in ((0, 0), (0, 1), (1, 1))]
        result = []
        for y in range(12):
            sums = [u[y], x1[y] + beside(u, y, 1), x2[y] + beside(u, y, 2), beside(x1, y, 1), beside(x2, y, 1) + beside(x1, y, 2)]
            here, up, down = [total([w * a for w, a in zip(by_dz[dz], sums)]) for dz in (0, -1, 1)]
            far = two[0] * sums[0] + two[1] * sums[1] + two[2] * sums[3]
            up = jnp.where(place8 == 3, jnp.where(last_row, 0.0, turn(turn(up, 3, 1), -1, 0)), turn(up, -1, 1))
            down = jnp.where(place8 == 0, jnp.where(first_row, 0.0, turn(turn(down, -3, 1), 1, 0)), turn(down, 1, 1))
            a, b = turn(far, 2, 1), turn(far, -2, 1)
            far = jnp.where(place8 >= 2, a + jnp.where(last_row, 0.0, turn(a, -1, 0)), b + jnp.where(first_row, 0.0, turn(b, 1, 0)))
            result.append(total([here, up, down, far]))
        return result

    def solve_level2(source):
        sides = level2_sides(source)
        residual = [KEEP * a + SIDE[2] * b for a, b in zip(source, sides)]
        source3 = []
        for y in range(6):
            pair = residual[2 * y] + residual[2 * y + 1]
            pair = pair + swapped(pair, 1)
            source3.append(0.125 * (pair + swapped(pair, 4)))
        pull = [PULL[3] * a for a in source3]
        iterate = pull
        for _ in range(SWEEPS - 1):
            sides = level3_sides(iterate)
            iterate = [KEEP * a + b + SIDE[3] * c for a, b, c in zip(iterate, pull, sides)]
        pull = [PULL[2] * a for a in source]
        u = [a + iterate[y // 2] for y, a in enumerate(pull)]
        sides = level2_sides(u)
        return [KEEP * a + b + SIDE[2] * c for a, b, c in zip(u, pull, sides)]

    def spread_level2(g, ds):
        row = 8 + s // 2
        a, b, c = [(e2, e2b)[g][pl.ds(row + by, MSG, stride=24), :] for by in (-1, 0, 1)]
        for d in ds:
            rows = a if d == -3 else jnp.where(odd == 1, b, a) if d < 0 else b if d < 2 else jnp.where(odd == 1, c, b) if d < 4 else c
            value = jnp.where(place16 == d % 4, rows, 0.0)
            value = value + swapped(value, 1)
            value = value + swapped(value, 2)
            pe2[g, d + 3, pl.ds(0, MSG, stride=2), :] = value
            pe2[g, d + 3, pl.ds(1, MSG, stride=2), :] = value

    even24 = (lanes(24) & 1) == 0

    def packed(a, b):
        return jnp.where(even24, a, b)

    def unpacked(value):
        return jnp.where(even24, value, turn(value, 1, 1)), jnp.where(even24, turn(value, -1, 1), value)

    def put_pe1(q, value):
        pe1[q + 4, pl.ds(8, 24, stride=2), :] = value
        pe1[q + 4, pl.ds(9, 24, stride=2), :] = value
        pe1[q + 4, 7:8, :] = value[23:24]
        pe1[q + 4, 56:57, :] = value[0:1]

    def correct_level1(g, reach):
        u = {q: pe2[g, q // 2 + 3, 0:24, :] for q in range(-reach - 1, 5 + reach)}
        return {
            q: KEEP * u[q] + (SIDE[1] * inside(q, 4)) * total([u[q - 1], u[q + 1], in_plane(u[q], 2)])
            for q in range(-reach, 4 + reach)
        }

    def base_level1(planes):
        answer = {}
        for q in planes:
            here = PULL[1] * f1[q + 3]
            sides = total([PULL[1] * f1[q + 2], PULL[1] * f1[q + 4], in_plane(here, 2)])
            answer[q] = (KEEP + 1.0) * here + (SIDE[1] * inside(q, 4)) * sides
        return answer

    def smooth(at, planes, plane, source):
        flag = inside(plane, 8)
        near = [at(p)[0] for p in (plane - 1, plane + 1) if p in planes]
        terms = []
        if plane in planes:
            here, before, after = at(plane)
            near += [before, after, turn(here, 1, 1) + turn(here, -1, 1)]
            terms.append(KEEP * here)
        if plane in source:
            terms.append((PULL[0] * flag) * f[plane + 3, 8:56, :])
        return total(terms + [(SIDE[0] * flag) * total(near)])

    def rows_at(ref, slot):
        return ref[slot, 8:56, :], ref[slot, 7:55, :], ref[slot, 9:57, :]

    def at_v2(p):
        return rows_at(v2, p + 4)

    def at_v(p):
        return rows_at(v, p + 6)

    def at_v1(p):
        return rows_at(v1, p + 6)

    def at_coarse(p):
        return rows_at(pe1, p // 2 + 4)

    def residual_mean(q, planes, source):
        pair = [fine_rows(v1, p + 6) for p in (2 * q, 2 * q + 1) if p in planes]
        beyond = [fine_rows(v1, p + 6) for p in (2 * q - 1, 2 * q + 2) if p in planes]
        rows = [fine_rows(f, p + 3)[:2] for p in (2 * q, 2 * q + 1) if p in source]
        return restricted(pair, beyond, rows, -CENTRE[0], STEP[0], 1)

    slab = range(8)
    for q in range(-1, 5):
        pair = [fine_rows(f, p + 3) for p in (2 * q, 2 * q + 1) if p in slab]
        beyond = [fine_rows(f, p + 3) for p in (2 * q - 1, 2 * q + 2) if p in slab]
        put_src1(q + 4, restricted(pair, beyond, [], KEEP, SIDE[0] * inside(q, 4), 1))
    send_first(level2_parts(range(-1, 5), range(-1, 3)))
    parts = {q: src1[q + 4, 8:32, :] for q in range(-1, 5)}
    for i in range(3):
        f1_out[i] = packed(parts[2 * i - 1], parts[2 * i])
    @pl.when(core == 1)
    def _():
        for copy in to_before:
            copy.start()

    @pl.when(core == 0)
    def _():
        orb_n[...] = orb_x[...]
        occ_n[...] = occ_x[...]

    below2, above2 = lax.rem(s + n_slab - 2, n_slab), lax.rem(s + 2, n_slab)
    send(f1_out.at[pl.ds(0, 2)], f1_in.at[pl.ds(2, 2)], f1_send.at[0], f1_recv.at[0], at_slab(below))
    send(f1_out.at[pl.ds(1, 2)], f1_in.at[pl.ds(0, 2)], f1_send.at[1], f1_recv.at[1], at_slab(above))

    send(f.at[pl.ds(3, 3), pl.ds(8, NY)], f.at[pl.ds(11, 3), pl.ds(8, NY)], f_send.at[0], f_recv.at[0], at_slab(below))
    send(f.at[pl.ds(8, 3), pl.ds(8, NY)], f.at[pl.ds(0, 3), pl.ds(8, NY)], f_send.at[1], f_recv.at[1], at_slab(above))
    faces = pending[2:4]
    pulled = {q: PULL[1] * parts[q] for q in parts}
    for q in range(-2, 6):
        near = [pulled.get(q - 1), pulled.get(q + 1)]
        terms = []
        if q in parts:
            near.append(in_plane(pulled[q], 2))
            terms = [(KEEP + 1.0) * pulled[q]]
        put_pe1(q, total(terms + [(SIDE[1] * inside(q, 4)) * total(near)]))
    for p in range(-4, 12):
        put(v2, p + 4, PULL[0] * f[p + 3, 8:56, :] + at_coarse(p)[0] if p in slab else at_coarse(p)[0])
    for p in range(-5, 13):
        put(v, p + 6, smooth(at_v2, range(-4, 12), p, slab))
    for p in range(-6, 14):
        put(v1, p + 6, smooth(at_v, range(-5, 13), p, slab))
    for q in range(-4, 8):
        put_src1(q + 4, inside(q, 4) * residual_mean(q, range(-6, 14), slab))
    shares = {q: src1[q + 4, 8:32, :] for q in (-4, -3, -2, -1, 2, 3, 0, 1, 4, 5, 6, 7)}
    for i, q in enumerate((-4, 0, 2, 6)):
        f2_out[i] = packed(shares[q], shares[q + 1])
    for i, device in enumerate((below2, below, above, above2)):
        send(f2_out.at[i], f2_in.at[i], f1_send.at[2 + i], f1_recv.at[2 + i], at_slab(device))
    send_second(level2_parts(range(-4, 8), range(-3, 5)))

    pending[0].wait_recv()
    pending[1].wait_recv()
    under = [low * plane for i in range(2) for plane in unpacked(f1_in[i])]
    over = [high * plane for i in range(2, 4) for plane in unpacked(f1_in[i])]
    mixed = {q: [part] for q, part in parts.items()}
    for first_plane, planes in ((-3, under), (3, over)):
        for i, plane in enumerate(planes):
            mixed.setdefault(first_plane + i, []).append(plane)
    for q in range(-3, 7):
        f1[q + 3] = total(mixed[q])
    base = base_level1(range(-2, 6))
    for q in base:
        e1[q + 2] = base[q]

    gathered(0).wait_recv()
    first = solve_level2(first_source())
    for y in range(12):
        e2[24 * y + 8 : 24 * y + 16, :] = first[y]
    spread_level2(0, range(-3, 5))
    answer1 = correct_level1(0, 4)
    for q in range(-2, 6):
        put_pe1(q, answer1[q] + e1[q + 2])
    for face in faces:
        face.wait_recv()
    for p in range(-3, 11):
        put(v2, p + 4, (PULL[0] * inside(p, 8)) * f[p + 3, 8:56, :] + at_coarse(p)[0])
    for p in range(-2, 10):
        put(v, p + 6, smooth(at_v2, range(-3, 11), p, range(-3, 11)))
    for p in range(-1, 9):
        put(v1, p + 6, smooth(at_v, range(-2, 10), p, range(-3, 11)))
    weight_x = -occ_x[0:1, :]
    to_x = []
    for h in range(4):
        for p in range(2 * h, 2 * h + 2):
            last[p] = smooth(at_v1, range(-1, 9), p, slab)
            both_x[0, p] = (last[p] * weight_x) * orb_x[p]
        planes = pl.ds(2 * h, 2)
        to_x.append(remote(both_x.at[0, planes], both_x.at[1, planes], prev_send.at[h], prev_recv.at[h], before))

        @pl.when(core == 1)
        def _():
            to_x[h].start()

    for q in range(4):
        f1[q + 3] = residual_mean(q, range(-1, 9), slab)

    answer = response(first)
    for q in answer1:
        put_pe1(q, answer1[q])
    for lowest in (-6, 6):
        for p in range(lowest, lowest + 8):
            put(v, p + 6, smooth(at_coarse, range(-8, 16), p, ()))
        for p in range(lowest + 1, lowest + 7):
            put(v1, p + 6, smooth(at_v, range(lowest, lowest + 8), p, ()))
    own_part = {q: inside(q, 4) * residual_mean(q, range(-6, 14), ()) for q in (-2, -1, 4, 5)}
    for copy in pending[4:8]:
        copy.wait_recv()
    gathered(1).wait_recv()
    second = solve_level2([a + b for a, b in zip(answer, second_source())])
    for y in range(12):
        e2b[24 * y + 8 : 24 * y + 16, :] = second[y]
    for q, near, far, near_flag, far_flag in ((-2, 2, 3, low, low2), (4, 1, 0, high, high2)):
        for i, (a, b) in enumerate(zip(unpacked(f2_in[near]), unpacked(f2_in[far]))):
            f1[q + i + 3] = total([shares[q + i], own_part[q + i], near_flag * a, far_flag * b])
    spread_level2(1, range(-1, 3))
    answer1 = correct_level1(1, 1)
    base = base_level1(range(-1, 5))
    fixes = {q: answer1[q] + base[q] for q in answer1}
    for i in range(3):
        fix_out[i] = packed(fixes[2 * i - 1], fixes[2 * i])
    fix_copy = remote(fix_out, fix_in, before_send.at[2], before_recv.at[2], before)

    @pl.when(core == 1)
    def _():
        fix_copy.start()

    @pl.when(core == 0)
    def _():
        fix_in[...] = fix_out[...]

    for q in fixes:
        put_pe1(q, fixes[q])

    @pl.when(core == 1)
    def _():
        to_next[1].wait_recv()

    weight_y = -occ_y[0:1, :]
    to_y = []
    for h in range(4):
        for p in range(2 * h, 2 * h + 2):
            potential = last[p] + smooth(at_coarse, range(-2, 10), p, ())
            out_y[p] = (potential * weight_y) * orb_y[p]
        planes = pl.ds(2 * h, 2)
        to_y.append(remote(out_y.at[planes], in_y.at[planes], ret_send.at[h], ret_recv.at[h], partner))
        to_y[h].start()

    @pl.when(core == 1)
    def _():
        for copy in to_before + to_x:
            copy.wait_recv()
        fix_copy.wait_recv()

    for i in range(3):
        for q, plane in zip((2 * i - 1, 2 * i), unpacked(fix_in[i])):
            put_pe1(q, plane)
    weight_n = -occ_n[0:1, :]
    for p in range(8):
        both_x[core, p] = both_x[core, p] + (smooth(at_coarse, range(-2, 10), p, ()) * weight_n) * orb_n[p]
    for h in range(4):
        to_y[h].wait_recv()
        for p in range(2 * h, 2 * h + 2):
            out_ref[0, p] = in_y[p] + both_x[core, p]

    for copy in to_partner + pending + to_y:
        copy.wait_send()
    for g in range(2):
        gathered(g).wait_send()

    @pl.when(core == 1)
    def _():
        for copy in to_next + to_x + to_before + [fix_copy]:
            copy.wait_send()


def on_device(n_orb, n_slab, orbitals, occupations):
    vmem, dma = pltpu.VMEM, pltpu.SemaphoreType.DMA
    f32 = jnp.float32

    def fine(planes):
        return vmem((planes, NY, NX), f32)

    def tall(planes):
        return vmem((planes, FINE, NX), f32)

    return pl.pallas_call(
        functools.partial(kernel, n_orb, n_slab),
        out_shape=jax.ShapeDtypeStruct(orbitals.shape, f32),
        in_specs=[pl.BlockSpec(memory_space=pltpu.SMEM), pl.BlockSpec(memory_space=pltpu.HBM)],
        out_specs=pl.BlockSpec(memory_space=pltpu.VMEM),
        scratch_shapes=[
            fine(8), fine(8), fine(8), vmem((8, 128), f32), vmem((8, 128), f32), vmem((8, 128), f32),
            tall(14), tall(16), tall(20), tall(20), tall(12),
            vmem((10, 24, 128), f32), vmem((12, ROWS1, 128), f32), vmem((2, 8, 32, 128), f32), vmem((8, 24, 128), f32),
            vmem((3, 24, 128), f32), vmem((4, 24, 128), f32), vmem((4, 24, 128), f32), vmem((4, 24, 128), f32), vmem((MSG2, 128), f32),
            vmem((18 * MSG, 128), f32), vmem((20 * MSG2, 128), f32), vmem((24 * 16, 128), f32), vmem((24 * 16, 128), f32),
            fine(8), fine(8), vmem((2, 8, NY, NX), f32),
            fine(8), vmem((8, 128), f32), fine(8), vmem((3, 24, 128), f32), vmem((3, 24, 128), f32),
            pltpu.SemaphoreType.REGULAR, dma, dma((2,)), dma((2,)), dma((2,)), dma((2,)), dma((2,)), dma((2,)), dma((6,)), dma((6,)), dma((2,)), dma((2,)),
            dma((4,)), dma((4,)), dma((4,)), dma((4,)), dma((3,)), dma((3,)),
        ],
        compiler_params=pltpu.CompilerParams(collective_id=0, has_side_effects=True, vmem_limit_bytes=32 * 2**20),
    )(occupations, pltpu.with_memory_space_constraint(orbitals, pltpu.HBM))


def solution(mesh):
    return jax.shard_map(
        functools.partial(on_device, mesh.shape["orb"], mesh.shape["slab"]),
        mesh=mesh,
        in_specs=(P("orb", "slab", None, None), P("orb")),
        out_specs=P("orb", "slab", None, None),
        check_vma=False,
    )
```

```python
import functools

import jax
import jax.numpy as jnp
import numpy as np
from jax import lax
from jax.experimental import pallas as pl
from jax.experimental.pallas import tpu as pltpu
from jax.sharding import PartitionSpec as P

MESH = pl.DeviceIdType.MESH

NZ, NY, NX = 128, 48, 128
SWEEPS = 6
screening = 0.001
relaxation = 0.8

STEP = [0.25**level for level in range(4)]
CENTRE = [6.0 * step + screening for step in STEP]
KEEP = 1.0 - relaxation
PULL = [relaxation / centre for centre in CENTRE]
SIDE = [pull * step for pull, step in zip(PULL, STEP)]

ROWS1 = 48
FINE = 64
MSG = 16
MSG2 = 24


def response_weights():
    def sides(u):
        padded = np.pad(u, ((0, 0), (1, 1), (0, 0), (0, 0)))
        return padded[:, 2:] + padded[:, :-2] + sum(np.roll(u, by, axis) for by in (1, -1) for axis in (2, 3))

    def smoothed(u, level):
        return KEEP * u + SIDE[level] * sides(u)

    def mean(u):
        b, z, y, x = u.shape
        return u.reshape(b, z // 2, 2, y // 2, 2, x // 2, 2).mean((2, 4, 6))

    def spread(u):
        return u.repeat(2, 1).repeat(2, 2).repeat(2, 3)

    unit = np.zeros((8, 8, 6, 6))
    for z in range(8):
        unit[z, z, 0, 0] = 1.0
    u = spread(smoothed(spread(unit), 1))
    u = smoothed(smoothed(u, 0), 0)
    u = mean(STEP[0] * sides(u) - CENTRE[0] * u)
    u = mean(smoothed(u, 1))
    weights = np.zeros((8, 5, 3, 3))
    for z in range(8):
        for dz in range(-2, 3):
            if 0 <= z + dz < 8:
                weights[z, dz + 2] = u[z, z + dz, :3, :3]
    return weights


def turn(value, by, axis):
    return pltpu.roll(value, by % value.shape[axis], axis)


def put(ref, slot, value):
    ref[slot, 8:56, :] = value
    ref[slot, 7:8, :] = value[47:48]
    ref[slot, 56:57, :] = value[0:1]


def lanes(rows):
    return lax.broadcasted_iota(jnp.int32, (rows, 128), 1)


def in_plane(value, lane_step):
    return (turn(value, 1, 0) + turn(value, -1, 0)) + (turn(value, lane_step, 1) + turn(value, -lane_step, 1))


def swapped(value, bit):
    first = (lanes(value.shape[0]) & bit) == 0
    return jnp.where(first, turn(value, -bit, 1), turn(value, bit, 1))


def total(parts):
    parts = [part for part in parts if part is not None]
    while len(parts) > 1:
        parts = [a + b for a, b in zip(parts[::2], parts[1::2])] + parts[len(parts) // 2 * 2 :]
    return parts[0] if parts else None


def kernel(
    n_orb, n_slab,
    occ_ref, orb_ref, out_ref,
    own, orb_x, orb_y, occ_own, occ_x, occ_y, f, v2, v, v1, pe1, f1, src1, pe2, e1, f1_out, f1_in, f2_out, f2_in, msg2, gather, gather2, e2, e2b,
    out_y, in_y, both_x, orb_n, occ_n, last, fix_out, fix_in,
    go, local_sem, orb_send, orb_recv, next_send, next_recv, gat_send, gat_recv, f1_send, f1_recv, f_send, f_recv, ret_send, ret_recv, prev_send, prev_recv, before_send, before_recv,
):
    o, s = lax.axis_index("orb"), lax.axis_index("slab")
    core = lax.rem(o, 2)
    partner = {"orb": o + 1 - 2 * core}
    before = {"orb": lax.rem(o + n_orb - 1 - core, n_orb)}
    after = {"orb": lax.rem(o + 2 - o // (n_orb - 1), n_orb)}
    start, home = o == 0, o == 1
    leads = (core == 1) & (o != 1) | (o == 0)
    above, below = lax.rem(s + 1, n_slab), lax.rem(s + n_slab - 1, n_slab)
    odd = lax.rem(s, 2)

    def at_slab(index):
        return {"slab": index}

    mine = pltpu.make_async_copy(orb_ref.at[0], own, local_sem)
    mine.start()
    peers = sorted(((x, y) for x in range(4) for y in range(4) if x or y), key=lambda d: -min(d[0], 4 - d[0]) - min(d[1], 4 - d[1]))
    peers = [4 * lax.rem(s // 4 + y, 4) + lax.rem(s + x, 4) for x, y in peers]

    barrier = pltpu.get_barrier_semaphore()

    def greet(device):
        pl.semaphore_signal(barrier, inc=1, device_id=device, device_id_type=MESH)

    greet(partner)

    @pl.when(core == 0)
    def _():
        for peer in peers:
            greet({"orb": o, "slab": peer})

    @pl.when(leads)
    def _():
        greet(before)

    @pl.when(core == 1)
    def _():
        greet({"orb": lax.rem(o + 1, n_orb)})
        for peer in peers:
            greet({"orb": o - 1, "slab": peer})

    occ_own[...] = jnp.full((8, 128), occ_ref[0], jnp.float32)
    for slot in (0, 17):
        gather[pl.ds(slot * MSG, MSG), :] = jnp.zeros((MSG, 128), jnp.float32)
    for slot in (0, 18):
        gather2[pl.ds(slot * MSG2, 2 * MSG2), :] = jnp.zeros((2 * MSG2, 128), jnp.float32)
    e2[...] = jnp.zeros_like(e2)
    e2b[...] = jnp.zeros_like(e2b)
    src1[...] = jnp.zeros_like(src1)
    low = jnp.where(s > 0, 1.0, 0.0).astype(jnp.float32)
    high = jnp.where(s < n_slab - 1, 1.0, 0.0).astype(jnp.float32)
    low2 = jnp.where(s > 1, 1.0, 0.0).astype(jnp.float32)
    high2 = jnp.where(s < n_slab - 2, 1.0, 0.0).astype(jnp.float32)

    def inside(plane, count):
        return low if plane < 0 else high if plane >= count else 1.0

    def remote(src, dst, send_sem, recv_sem, device):
        return pltpu.make_async_remote_copy(src, dst, send_sem, recv_sem, device_id=device, device_id_type=MESH)

    mine.wait()

    @pl.when(core == 0)
    def _():
        pl.semaphore_wait(barrier, 2 * n_slab)
        pl.semaphore_signal(go, inc=1, device_id=partner, device_id_type=MESH)

    @pl.when(core == 1)
    def _():
        pl.semaphore_wait(barrier, 2)

    to_next = [
        remote(own, orb_y, next_send.at[0], next_recv.at[0], after),
        remote(occ_own, occ_y, next_send.at[1], next_recv.at[1], after),
    ]
    to_partner = [
        remote(own, orb_x, orb_send.at[0], orb_recv.at[0], partner),
        remote(occ_own, occ_x, orb_send.at[1], orb_recv.at[1], partner),
    ]

    @pl.when(core == 1)
    def _():
        for copy in to_next:
            copy.start()

    @pl.when(jnp.logical_not(home))
    def _():
        for copy in to_partner:
            copy.start()

    @pl.when(start)
    def _():
        occ_x[...] = occ_own[...]
        orb_x[...] = own[...]

    @pl.when(jnp.logical_not(leads))
    def _():
        occ_y[...] = occ_own[...]
        orb_y[...] = own[...]

    @pl.when(jnp.logical_not(start))
    def _():
        for copy in to_partner:
            copy.wait_recv()

    @pl.when(leads)
    def _():
        for copy in to_next:
            copy.wait_recv()

    for p in range(8):
        put(f, 3 + p, orb_x[p] * orb_y[p])

    to_before = [
        remote(orb_x, orb_n, before_send.at[0], before_recv.at[0], before),
        remote(occ_x, occ_n, before_send.at[1], before_recv.at[1], before),
    ]

    pending = []

    def send(src, dst, send_sem, recv_sem, device):
        copy = remote(src, dst, send_sem, recv_sem, device)
        copy.start()
        pending.append(copy)
        return copy

    def restricted(pair, beyond, source, centre, side, bit):
        beyond = total([part for plane in beyond for part in plane[:2]])
        terms = []
        if pair:
            even, odd_, before, after = [total([plane[i] for plane in pair]) for i in range(4)]
            both = even + odd_
            terms.append(centre * both)
            around = total([both + both, before, after, turn(both, bit, 1), turn(both, -bit, 1), beyond])
        else:
            around = beyond
        terms.append(side * around)
        terms += [part for plane in source for part in plane]
        mean = total(terms)
        return 0.125 * (mean + swapped(mean, bit))

    def fine_rows(ref, plane):
        return [ref[plane, pl.ds(8 + start, 24, stride=2), :] for start in (0, 1, -1, 2)]

    def put_src1(slot, value):
        src1[slot, 8:32, :] = value
        src1[slot, 7:8, :] = value[23:24]
        src1[slot, 32:33, :] = value[0:1]

    def coarse_rows(slot):
        return [src1[slot, pl.ds(8 + start, MSG, stride=2), :] for start in (0, 1, -1, 2)]

    lane16 = lanes(MSG)
    place16 = (lane16 + 2 * odd) & 3

    def level2_parts(have, planes):
        parts = {}
        for d in planes:
            pair = [coarse_rows(q + 4) for q in (2 * d, 2 * d + 1) if q in have]
            beyond = [coarse_rows(q + 4) for q in (2 * d - 1, 2 * d + 2) if q in have]
            parts[d] = restricted(pair, beyond, [], KEEP, SIDE[1], 2)
        return parts

    def laid(parts, planes):
        by_place = {d % 4: parts[d] for d in planes}
        return jnp.where(place16 < 2, jnp.where(place16 == 0, by_place[0], by_place[1]), jnp.where(place16 == 2, by_place[2], by_place[3]))

    slot1 = pl.ds(pl.multiple_of((s + 1) * MSG, MSG), MSG)
    slot2 = pl.ds(pl.multiple_of((s + 2) * MSG2, MSG2), MSG2)

    def send_first(parts):
        gather[slot1, :] = laid(parts, range(-1, 3))

        @pl.when(core == 1)
        def _():
            pl.semaphore_wait(go, 1)

        for peer in peers:
            remote(gather.at[slot1], gather.at[slot1], gat_send.at[0], gat_recv.at[0], at_slab(peer)).start()

    def send_second(parts):
        msg2[0:12, :] = laid(parts, range(-1, 3))[0:12]
        msg2[12:24, :] = laid(parts, (-3, -2, 3, 4))[0:12]
        gather2[slot2, :] = msg2[...]
        for peer in peers:
            remote(msg2, gather2.at[slot2], gat_send.at[1], gat_recv.at[1], at_slab(peer)).start()

    def gathered(g):
        most = gather.at[pl.ds(0, (n_slab - 1) * MSG)] if g == 0 else gather2.at[pl.ds(0, (n_slab - 1) * MSG2)]
        return remote(most, most, gat_send.at[g], gat_recv.at[g], at_slab(above))

    row8 = lax.broadcasted_iota(jnp.int32, (8, 128), 0)
    lane8 = lanes(8)
    first_row, last_row = row8 == 0, row8 == 7

    def level2_sides(u):
        result = []
        for y in range(12):
            here = u[y]
            up = jnp.where(last_row, 0.0, turn(turn(here, 3, 1), -1, 0))
            down = jnp.where(first_row, 0.0, turn(turn(here, -3, 1), 1, 0))
            up = jnp.where((lane8 & 3) == 3, up, turn(here, -1, 1))
            down = jnp.where((lane8 & 3) == 0, down, turn(here, 1, 1))
            x = turn(here, 4, 1) + turn(here, -4, 1)
            result.append(total([u[(y + 1) % 12], u[(y + 11) % 12], up, down, x]))
        return result

    def level3_sides(u):
        result = []
        lower = (lane8 & 2) == 0
        for y in range(6):
            here = u[y]
            a, b = turn(here, -2, 1), turn(here, 2, 1)
            far = jnp.where(lower, jnp.where(first_row, 0.0, turn(a, 1, 0)), jnp.where(last_row, 0.0, turn(b, -1, 0)))
            x = turn(here, 8, 1) + turn(here, -8, 1)
            result.append(total([u[(y + 1) % 6], u[(y + 5) % 6], jnp.where(lower, a, b), far, x]))
        return result

    place8 = lane8 & 3

    def first_source():
        source = []
        for y in range(12):
            even, odd_, even_after, odd_before = [gather[pl.ds(MSG * k + y, 8, stride=2 * MSG), :] for k in (1, 2, 3, 0)]
            source.append(jnp.where(place8 == 3, even_after, even) + jnp.where(place8 == 0, odd_before, odd_))
        return source

    def second_source():
        source = []
        for y in range(12):
            even, odd_, even_after, odd_before = [gather2[pl.ds(MSG2 * k + y, 8, stride=2 * MSG2), :] for k in (2, 3, 4, 1)]
            near = jnp.where(place8 == 3, even_after, even) + jnp.where(place8 == 0, odd_before, odd_)
            even_before, even, even_after, odd_before, odd_, odd_after = [
                gather2[pl.ds(MSG2 * k + 12 + y, 8, stride=2 * MSG2), :] for k in (0, 2, 4, 1, 3, 5)]
            far = jnp.where(place8 == 0, even_before, jnp.where(place8 == 3, even, even_after))
            far = far + jnp.where(place8 == 0, odd_, jnp.where(place8 == 3, odd_after, odd_before))
            source.append(near + far)
        return source

    def response(u):
        weights = response_weights()
        plane = 4 * row8 + place8

        def weight(dz, dy, dx):
            inner = float(weights[4, dz + 2, dy, dx])
            value = inner
            for at, z in ((0, 0), (1, 1), (30, 6), (31, 7)):
                if abs(weights[z, dz + 2, dy, dx] - inner) > 1e-12:
                    value = jnp.where(plane == at, jnp.float32(weights[z, dz + 2, dy, dx]), value)
            return value

        x1 = [turn(a, 4, 1) + turn(a, -4, 1) for a in u]
        x2 = [turn(a, 8, 1) + turn(a, -8, 1) for a in u]

        def beside(a, y, by):
            return a[(y + by) % 12] + a[(y - by) % 12]

        groups = ((0, 0), (0, 1), (0, 2), (1, 1), (1, 2))
        by_dz = {dz: [weight(dz, *group) for group in groups] for dz in (-1, 0, 1)}
        two = [float(weights[4, 4, dy, dx]) for dy, dx in ((0, 0), (0, 1), (1, 1))]
        result = []
        for y in range(12):
            sums = [u[y], x1[y] + beside(u, y, 1), x2[y] + beside(u, y, 2), beside(x1, y, 1), beside(x2, y, 1) + beside(x1, y, 2)]
            here, up, down = [total([w * a for w, a in zip(by_dz[dz], sums)]) for dz in (0, -1, 1)]
            far = two[0] * sums[0] + two[1] * sums[1] + two[2] * sums[3]
            up = jnp.where(place8 == 3, jnp.where(last_row, 0.0, turn(turn(up, 3, 1), -1, 0)), turn(up, -1, 1))
            down = jnp.where(place8 == 0, jnp.where(first_row, 0.0, turn(turn(down, -3, 1), 1, 0)), turn(down, 1, 1))
            a, b = turn(far, 2, 1), turn(far, -2, 1)
            far = jnp.where(place8 >= 2, a + jnp.where(last_row, 0.0, turn(a, -1, 0)), b + jnp.where(first_row, 0.0, turn(b, 1, 0)))
            result.append(total([here, up, down, far]))
        return result

    def solve_level2(source):
        sides = level2_sides(source)
        residual = [KEEP * a + SIDE[2] * b for a, b in zip(source, sides)]
        source3 = []
        for y in range(6):
            pair = residual[2 * y] + residual[2 * y + 1]
            pair = pair + swapped(pair, 1)
            source3.append(0.125 * (pair + swapped(pair, 4)))
        pull = [PULL[3] * a for a in source3]
        iterate = pull
        for _ in range(SWEEPS - 1):
            sides = level3_sides(iterate)
            iterate = [KEEP * a + b + SIDE[3] * c for a, b, c in zip(iterate, pull, sides)]
        pull = [PULL[2] * a for a in source]
        u = [a + iterate[y // 2] for y, a in enumerate(pull)]
        sides = level2_sides(u)
        return [KEEP * a + b + SIDE[2] * c for a, b, c in zip(u, pull, sides)]

    def spread_level2(g, ds):
        row = 8 + s // 2
        a, b, c = [(e2, e2b)[g][pl.ds(row + by, MSG, stride=24), :] for by in (-1, 0, 1)]
        for d in ds:
            rows = a if d == -3 else jnp.where(odd == 1, b, a) if d < 0 else b if d < 2 else jnp.where(odd == 1, c, b) if d < 4 else c
            value = jnp.where(place16 == d % 4, rows, 0.0)
            value = value + swapped(value, 1)
            value = value + swapped(value, 2)
            pe2[g, d + 3, pl.ds(0, MSG, stride=2), :] = value
            pe2[g, d + 3, pl.ds(1, MSG, stride=2), :] = value

    even24 = (lanes(24) & 1) == 0

    def packed(a, b):
        return jnp.where(even24, a, b)

    def unpacked(value):
        return jnp.where(even24, value, turn(value, 1, 1)), jnp.where(even24, turn(value, -1, 1), value)

    def put_pe1(q, value):
        pe1[q + 4, pl.ds(8, 24, stride=2), :] = value
        pe1[q + 4, pl.ds(9, 24, stride=2), :] = value
        pe1[q + 4, 7:8, :] = value[23:24]
        pe1[q + 4, 56:57, :] = value[0:1]

    def correct_level1(g, reach):
        u = {q: pe2[g, q // 2 + 3, 0:24, :] for q in range(-reach - 1, 5 + reach)}
        return {
            q: KEEP * u[q] + (SIDE[1] * inside(q, 4)) * total([u[q - 1], u[q + 1], in_plane(u[q], 2)])
            for q in range(-reach, 4 + reach)
        }

    def base_level1(planes):
        answer = {}
        for q in planes:
            here = PULL[1] * f1[q + 3]
            sides = total([PULL[1] * f1[q + 2], PULL[1] * f1[q + 4], in_plane(here, 2)])
            answer[q] = (KEEP + 1.0) * here + (SIDE[1] * inside(q, 4)) * sides
        return answer

    def smooth(at, planes, plane, source):
        flag = inside(plane, 8)
        near = [at(p)[0] for p in (plane - 1, plane + 1) if p in planes]
        terms = []
        if plane in planes:
            here, before, after = at(plane)
            near += [before, after, turn(here, 1, 1) + turn(here, -1, 1)]
            terms.append(KEEP * here)
        if plane in source:
            terms.append((PULL[0] * flag) * f[plane + 3, 8:56, :])
        return total(terms + [(SIDE[0] * flag) * total(near)])

    def rows_at(ref, slot):
        return ref[slot, 8:56, :], ref[slot, 7:55, :], ref[slot, 9:57, :]

    def at_v2(p):
        return rows_at(v2, p + 4)

    def at_v(p):
        return rows_at(v, p + 6)

    def at_v1(p):
        return rows_at(v1, p + 6)

    def at_coarse(p):
        return rows_at(pe1, p // 2 + 4)

    def residual_mean(q, planes, source):
        pair = [fine_rows(v1, p + 6) for p in (2 * q, 2 * q + 1) if p in planes]
        beyond = [fine_rows(v1, p + 6) for p in (2 * q - 1, 2 * q + 2) if p in planes]
        rows = [fine_rows(f, p + 3)[:2] for p in (2 * q, 2 * q + 1) if p in source]
        return restricted(pair, beyond, rows, -CENTRE[0], STEP[0], 1)

    slab = range(8)
    for q in range(-1, 5):
        pair = [fine_rows(f, p + 3) for p in (2 * q, 2 * q + 1) if p in slab]
        beyond = [fine_rows(f, p + 3) for p in (2 * q - 1, 2 * q + 2) if p in slab]
        put_src1(q + 4, restricted(pair, beyond, [], KEEP, SIDE[0] * inside(q, 4), 1))
    send_first(level2_parts(range(-1, 5), range(-1, 3)))
    parts = {q: src1[q + 4, 8:32, :] for q in range(-1, 5)}
    for i in range(3):
        f1_out[i] = packed(parts[2 * i - 1], parts[2 * i])
    @pl.when(leads)
    def _():
        for copy in to_before:
            copy.start()

    @pl.when((core == 0) & (o != 0))
    def _():
        orb_n[...] = orb_x[...]
        occ_n[...] = occ_x[...]

    @pl.when(start)
    def _():
        orb_n[...] = orb_y[...]
        occ_n[...] = occ_y[...]

    below2, above2 = lax.rem(s + n_slab - 2, n_slab), lax.rem(s + 2, n_slab)
    send(f1_out.at[pl.ds(0, 2)], f1_in.at[pl.ds(2, 2)], f1_send.at[0], f1_recv.at[0], at_slab(below))
    send(f1_out.at[pl.ds(1, 2)], f1_in.at[pl.ds(0, 2)], f1_send.at[1], f1_recv.at[1], at_slab(above))

    send(f.at[pl.ds(3, 3), pl.ds(8, NY)], f.at[pl.ds(11, 3), pl.ds(8, NY)], f_send.at[0], f_recv.at[0], at_slab(below))
    send(f.at[pl.ds(8, 3), pl.ds(8, NY)], f.at[pl.ds(0, 3), pl.ds(8, NY)], f_send.at[1], f_recv.at[1], at_slab(above))
    faces = pending[2:4]
    pulled = {q: PULL[1] * parts[q] for q in parts}
    for q in range(-2, 6):
        near = [pulled.get(q - 1), pulled.get(q + 1)]
        terms = []
        if q in parts:
            near.append(in_plane(pulled[q], 2))
            terms = [(KEEP + 1.0) * pulled[q]]
        put_pe1(q, total(terms + [(SIDE[1] * inside(q, 4)) * total(near)]))
    for p in range(-4, 12):
        put(v2, p + 4, PULL[0] * f[p + 3, 8:56, :] + at_coarse(p)[0] if p in slab else at_coarse(p)[0])
    for p in range(-5, 13):
        put(v, p + 6, smooth(at_v2, range(-4, 12), p, slab))
    for p in range(-6, 14):
        put(v1, p + 6, smooth(at_v, range(-5, 13), p, slab))
    for q in range(-4, 8):
        put_src1(q + 4, inside(q, 4) * residual_mean(q, range(-6, 14), slab))
    shares = {q: src1[q + 4, 8:32, :] for q in (-4, -3, -2, -1, 2, 3, 0, 1, 4, 5, 6, 7)}
    for i, q in enumerate((-4, 0, 2, 6)):
        f2_out[i] = packed(shares[q], shares[q + 1])
    for i, device in enumerate((below2, below, above, above2)):
        send(f2_out.at[i], f2_in.at[i], f1_send.at[2 + i], f1_recv.at[2 + i], at_slab(device))
    send_second(level2_parts(range(-4, 8), range(-3, 5)))

    pending[0].wait_recv()
    pending[1].wait_recv()
    under = [low * plane for i in range(2) for plane in unpacked(f1_in[i])]
    over = [high * plane for i in range(2, 4) for plane in unpacked(f1_in[i])]
    mixed = {q: [part] for q, part in parts.items()}
    for first_plane, planes in ((-3, under), (3, over)):
        for i, plane in enumerate(planes):
            mixed.setdefault(first_plane + i, []).append(plane)
    for q in range(-3, 7):
        f1[q + 3] = total(mixed[q])
    base = base_level1(range(-2, 6))
    for q in base:
        e1[q + 2] = base[q]

    gathered(0).wait_recv()
    first = solve_level2(first_source())
    for y in range(12):
        e2[24 * y + 8 : 24 * y + 16, :] = first[y]
    answer = response(first)
    spread_level2(0, range(-3, 5))
    answer1 = correct_level1(0, 4)
    for q in range(-2, 6):
        put_pe1(q, answer1[q] + e1[q + 2])
    for face in faces:
        face.wait_recv()
    for p in range(-3, 11):
        put(v2, p + 4, (PULL[0] * inside(p, 8)) * f[p + 3, 8:56, :] + at_coarse(p)[0])
    for p in range(-2, 10):
        put(v, p + 6, smooth(at_v2, range(-3, 11), p, range(-3, 11)))
    for p in range(-1, 9):
        put(v1, p + 6, smooth(at_v, range(-2, 10), p, range(-3, 11)))
    weight_x = -occ_x[0:1, :]
    to_x = []
    for h in range(4):
        for p in range(2 * h, 2 * h + 2):
            last[p] = smooth(at_v1, range(-1, 9), p, slab)
            both_x[0, p] = (last[p] * weight_x) * orb_x[p]
        planes = pl.ds(2 * h, 2)
        to_x.append(remote(both_x.at[0, planes], both_x.at[1, planes], prev_send.at[h], prev_recv.at[h], before))

        @pl.when(leads)
        def _():
            to_x[h].start()

    @pl.when(start)
    def _():
        weight_y = -occ_y[0:1, :]
        for p in range(8):
            both_x[1, p] = (last[p] * weight_y) * orb_y[p]

    for q in range(4):
        f1[q + 3] = residual_mean(q, range(-1, 9), slab)

    for copy in pending[4:8]:
        copy.wait_recv()
    gathered(1).wait_recv()
    second = solve_level2([a + b for a, b in zip(answer, second_source())])
    for y in range(12):
        e2b[24 * y + 8 : 24 * y + 16, :] = second[y]
    for q in answer1:
        put_pe1(q, answer1[q])
    for lowest in (-6, 6):
        for p in range(lowest, lowest + 8):
            put(v, p + 6, smooth(at_coarse, range(-8, 16), p, ()))
        for p in range(lowest + 1, lowest + 7):
            put(v1, p + 6, smooth(at_v, range(lowest, lowest + 8), p, ()))
    own_part = {q: inside(q, 4) * residual_mean(q, range(-6, 14), ()) for q in (-2, -1, 4, 5)}
    for q, near, far, near_flag, far_flag in ((-2, 2, 3, low, low2), (4, 1, 0, high, high2)):
        for i, (a, b) in enumerate(zip(unpacked(f2_in[near]), unpacked(f2_in[far]))):
            f1[q + i + 3] = total([shares[q + i], own_part[q + i], near_flag * a, far_flag * b])
    spread_level2(1, range(-1, 3))
    answer1 = correct_level1(1, 1)
    base = base_level1(range(-1, 5))
    fixes = {q: answer1[q] + base[q] for q in answer1}
    for i in range(3):
        fix_out[i] = packed(fixes[2 * i - 1], fixes[2 * i])
    fix_copy = remote(fix_out, fix_in, before_send.at[2], before_recv.at[2], before)

    @pl.when(leads)
    def _():
        fix_copy.start()

    @pl.when(core == 0)
    def _():
        fix_in[...] = fix_out[...]

    for q in fixes:
        put_pe1(q, fixes[q])

    weight_y = -occ_y[0:1, :]
    to_y = []
    for h in range(4):
        for p in range(2 * h, 2 * h + 2):
            potential = last[p] + smooth(at_coarse, range(-2, 10), p, ())
            out_y[p] = (potential * weight_y) * orb_y[p]

            @pl.when(home)
            def _():
                in_y[p] = (potential * weight_x) * orb_x[p]

        planes = pl.ds(2 * h, 2)
        to_y.append(remote(out_y.at[planes], in_y.at[planes], ret_send.at[h], ret_recv.at[h], partner))

        @pl.when(jnp.logical_not(start))
        def _():
            to_y[h].start()

    @pl.when(core == 1)
    def _():
        for copy in to_before + to_x:
            copy.wait_recv()
        fix_copy.wait_recv()

    for i in range(3):
        for q, plane in zip((2 * i - 1, 2 * i), unpacked(fix_in[i])):
            put_pe1(q, plane)
    weight_n = -occ_n[0:1, :]
    kept = jnp.where(start, 1, core)
    for p in range(8):
        both_x[kept, p] = both_x[kept, p] + (smooth(at_coarse, range(-2, 10), p, ()) * weight_n) * orb_n[p]
    for h in range(4):

        @pl.when(jnp.logical_not(home))
        def _():
            to_y[h].wait_recv()

        for p in range(2 * h, 2 * h + 2):
            out_ref[0, p] = in_y[p] + both_x[kept, p]

    for copy in pending:
        copy.wait_send()

    @pl.when(jnp.logical_not(home))
    def _():
        for copy in to_partner:
            copy.wait_send()

    @pl.when(jnp.logical_not(start))
    def _():
        for copy in to_y:
            copy.wait_send()

    for g in range(2):
        gathered(g).wait_send()

    @pl.when(core == 1)
    def _():
        for copy in to_next:
            copy.wait_send()

    @pl.when(leads)
    def _():
        for copy in to_x + to_before + [fix_copy]:
            copy.wait_send()


def on_device(n_orb, n_slab, orbitals, occupations):
    vmem, dma = pltpu.VMEM, pltpu.SemaphoreType.DMA
    f32 = jnp.float32

    def fine(planes):
        return vmem((planes, NY, NX), f32)

    def tall(planes):
        return vmem((planes, FINE, NX), f32)

    return pl.pallas_call(
        functools.partial(kernel, n_orb, n_slab),
        out_shape=jax.ShapeDtypeStruct(orbitals.shape, f32),
        in_specs=[pl.BlockSpec(memory_space=pltpu.SMEM), pl.BlockSpec(memory_space=pltpu.HBM)],
        out_specs=pl.BlockSpec(memory_space=pltpu.VMEM),
        scratch_shapes=[
            fine(8), fine(8), fine(8), vmem((8, 128), f32), vmem((8, 128), f32), vmem((8, 128), f32),
            tall(14), tall(16), tall(20), tall(20), tall(12),
            vmem((10, 24, 128), f32), vmem((12, ROWS1, 128), f32), vmem((2, 8, 32, 128), f32), vmem((8, 24, 128), f32),
            vmem((3, 24, 128), f32), vmem((4, 24, 128), f32), vmem((4, 24, 128), f32), vmem((4, 24, 128), f32), vmem((MSG2, 128), f32),
            vmem((18 * MSG, 128), f32), vmem((20 * MSG2, 128), f32), vmem((24 * 16, 128), f32), vmem((24 * 16, 128), f32),
            fine(8), fine(8), vmem((2, 8, NY, NX), f32),
            fine(8), vmem((8, 128), f32), fine(8), vmem((3, 24, 128), f32), vmem((3, 24, 128), f32),
            pltpu.SemaphoreType.REGULAR, dma, dma((2,)), dma((2,)), dma((2,)), dma((2,)), dma((2,)), dma((2,)), dma((6,)), dma((6,)), dma((2,)), dma((2,)),
            dma((4,)), dma((4,)), dma((4,)), dma((4,)), dma((3,)), dma((3,)),
        ],
        compiler_params=pltpu.CompilerParams(collective_id=0, has_side_effects=True, vmem_limit_bytes=32 * 2**20),
    )(occupations, pltpu.with_memory_space_constraint(orbitals, pltpu.HBM))


def solution(mesh):
    return jax.shard_map(
        functools.partial(on_device, mesh.shape["orb"], mesh.shape["slab"]),
        mesh=mesh,
        in_specs=(P("orb", "slab", None, None), P("orb")),
        out_specs=P("orb", "slab", None, None),
        check_vma=False,
    )
```

```python
import functools

import jax
import jax.numpy as jnp
import numpy as np
from jax import lax
from jax.experimental import pallas as pl
from jax.experimental.pallas import tpu as pltpu
from jax.sharding import PartitionSpec as P

MESH = pl.DeviceIdType.MESH

NZ, NY, NX = 128, 48, 128
SWEEPS = 6
screening = 0.001
relaxation = 0.8

STEP = [0.25**level for level in range(4)]
CENTRE = [6.0 * step + screening for step in STEP]
KEEP = 1.0 - relaxation
PULL = [relaxation / centre for centre in CENTRE]
SIDE = [pull * step for pull, step in zip(PULL, STEP)]

ROWS1 = 48
FINE = 64
MSG = 16
MSG2 = 24


def response_weights():
    def sides(u):
        padded = np.pad(u, ((0, 0), (1, 1), (0, 0), (0, 0)))
        return padded[:, 2:] + padded[:, :-2] + sum(np.roll(u, by, axis) for by in (1, -1) for axis in (2, 3))

    def smoothed(u, level):
        return KEEP * u + SIDE[level] * sides(u)

    def mean(u):
        b, z, y, x = u.shape
        return u.reshape(b, z // 2, 2, y // 2, 2, x // 2, 2).mean((2, 4, 6))

    def spread(u):
        return u.repeat(2, 1).repeat(2, 2).repeat(2, 3)

    unit = np.zeros((8, 8, 6, 6))
    for z in range(8):
        unit[z, z, 0, 0] = 1.0
    u = spread(smoothed(spread(unit), 1))
    u = smoothed(smoothed(u, 0), 0)
    u = mean(STEP[0] * sides(u) - CENTRE[0] * u)
    u = mean(smoothed(u, 1))
    weights = np.zeros((8, 5, 3, 3))
    for z in range(8):
        for dz in range(-2, 3):
            if 0 <= z + dz < 8:
                weights[z, dz + 2] = u[z, z + dz, :3, :3]
    return weights


def turn(value, by, axis):
    return pltpu.roll(value, by % value.shape[axis], axis)


def put(ref, slot, value):
    ref[slot, 8:56, :] = value
    ref[slot, 7:8, :] = value[47:48]
    ref[slot, 56:57, :] = value[0:1]


def lanes(rows):
    return lax.broadcasted_iota(jnp.int32, (rows, 128), 1)


def in_plane(value, lane_step):
    return (turn(value, 1, 0) + turn(value, -1, 0)) + (turn(value, lane_step, 1) + turn(value, -lane_step, 1))


def swapped(value, bit):
    first = (lanes(value.shape[0]) & bit) == 0
    return jnp.where(first, turn(value, -bit, 1), turn(value, bit, 1))


def total(parts):
    parts = [part for part in parts if part is not None]
    while len(parts) > 1:
        parts = [a + b for a, b in zip(parts[::2], parts[1::2])] + parts[len(parts) // 2 * 2 :]
    return parts[0] if parts else None


def kernel(
    n_orb, n_slab,
    occ_ref, orb_ref, out_ref,
    own, orb_x, orb_y, occ_own, occ_x, occ_y, f, v2, v, v1, pe1, f1, src1, pe2, e1, f1_out, f1_in, f2_out, f2_in, msg2, gather, gather2, e2, e2b,
    out_y, in_y, both_x, orb_n, occ_n, last, fix_out, fix_in,
    go, local_sem, orb_send, orb_recv, next_send, next_recv, gat_send, gat_recv, f1_send, f1_recv, f_send, f_recv, ret_send, ret_recv, prev_send, prev_recv, before_send, before_recv,
):
    o, s = lax.axis_index("orb"), lax.axis_index("slab")
    core = lax.rem(o, 2)
    partner = {"orb": o + 1 - 2 * core}
    before = {"orb": lax.rem(o + n_orb - 1 - core, n_orb)}
    after = {"orb": lax.rem(o + 2 - o // (n_orb - 1), n_orb)}
    start, home = o == 0, o == 1
    leads = (core == 1) & (o != 1) | (o == 0)
    above, below = lax.rem(s + 1, n_slab), lax.rem(s + n_slab - 1, n_slab)
    odd = lax.rem(s, 2)

    def at_slab(index):
        return {"slab": index}

    mine = pltpu.make_async_copy(orb_ref.at[0], own, local_sem)
    mine.start()
    peers = sorted(((x, y) for x in range(4) for y in range(4) if x or y), key=lambda d: -min(d[0], 4 - d[0]) - min(d[1], 4 - d[1]))
    peers = [4 * lax.rem(s // 4 + y, 4) + lax.rem(s + x, 4) for x, y in peers]

    barrier = pltpu.get_barrier_semaphore()

    def greet(device):
        pl.semaphore_signal(barrier, inc=1, device_id=device, device_id_type=MESH)

    greet(partner)

    @pl.when(core == 0)
    def _():
        for peer in peers:
            greet({"orb": o, "slab": peer})

    @pl.when(leads)
    def _():
        greet(before)

    @pl.when(core == 1)
    def _():
        greet({"orb": lax.rem(o + 1, n_orb)})
        for peer in peers:
            greet({"orb": o - 1, "slab": peer})

    occ_own[...] = jnp.full((8, 128), occ_ref[0], jnp.float32)
    for slot in (0, 17):
        gather[pl.ds(slot * MSG, MSG), :] = jnp.zeros((MSG, 128), jnp.float32)
    for slot in (0, 18):
        gather2[pl.ds(slot * MSG2, 2 * MSG2), :] = jnp.zeros((2 * MSG2, 128), jnp.float32)
    e2[...] = jnp.zeros_like(e2)
    e2b[...] = jnp.zeros_like(e2b)
    src1[...] = jnp.zeros_like(src1)
    low = jnp.where(s > 0, 1.0, 0.0).astype(jnp.float32)
    high = jnp.where(s < n_slab - 1, 1.0, 0.0).astype(jnp.float32)
    low2 = jnp.where(s > 1, 1.0, 0.0).astype(jnp.float32)
    high2 = jnp.where(s < n_slab - 2, 1.0, 0.0).astype(jnp.float32)

    def inside(plane, count):
        return low if plane < 0 else high if plane >= count else 1.0

    def remote(src, dst, send_sem, recv_sem, device):
        return pltpu.make_async_remote_copy(src, dst, send_sem, recv_sem, device_id=device, device_id_type=MESH)

    mine.wait()

    @pl.when(core == 0)
    def _():
        pl.semaphore_wait(barrier, 2 * n_slab)
        pl.semaphore_signal(go, inc=1, device_id=partner, device_id_type=MESH)

    @pl.when(core == 1)
    def _():
        pl.semaphore_wait(barrier, 2)

    to_next = [
        remote(own, orb_y, next_send.at[0], next_recv.at[0], after),
        remote(occ_own, occ_y, next_send.at[1], next_recv.at[1], after),
    ]
    to_partner = [
        remote(own, orb_x, orb_send.at[0], orb_recv.at[0], partner),
        remote(occ_own, occ_x, orb_send.at[1], orb_recv.at[1], partner),
    ]

    @pl.when(core == 1)
    def _():
        for copy in to_next:
            copy.start()

    @pl.when(jnp.logical_not(home))
    def _():
        for copy in to_partner:
            copy.start()

    @pl.when(start)
    def _():
        occ_x[...] = occ_own[...]
        orb_x[...] = own[...]

    @pl.when(jnp.logical_not(leads))
    def _():
        occ_y[...] = occ_own[...]
        orb_y[...] = own[...]

    @pl.when(jnp.logical_not(start))
    def _():
        for copy in to_partner:
            copy.wait_recv()

    @pl.when(leads)
    def _():
        for copy in to_next:
            copy.wait_recv()

    for p in range(8):
        put(f, 3 + p, orb_x[p] * orb_y[p])

    to_before = [
        remote(orb_x, orb_n, before_send.at[0], before_recv.at[0], before),
        remote(occ_x, occ_n, before_send.at[1], before_recv.at[1], before),
    ]

    pending = []

    def send(src, dst, send_sem, recv_sem, device):
        copy = remote(src, dst, send_sem, recv_sem, device)
        copy.start()
        pending.append(copy)
        return copy

    def restricted(pair, beyond, source, centre, side, bit):
        beyond = total([part for plane in beyond for part in plane[:2]])
        terms = []
        if pair:
            even, odd_, before, after = [total([plane[i] for plane in pair]) for i in range(4)]
            both = even + odd_
            terms.append(centre * both)
            around = total([both + both, before, after, turn(both, bit, 1), turn(both, -bit, 1), beyond])
        else:
            around = beyond
        terms.append(side * around)
        terms += [part for plane in source for part in plane]
        mean = total(terms)
        return 0.125 * (mean + swapped(mean, bit))

    def fine_rows(ref, plane):
        return [ref[plane, pl.ds(8 + start, 24, stride=2), :] for start in (0, 1, -1, 2)]

    def put_src1(slot, value):
        src1[slot, 8:32, :] = value
        src1[slot, 7:8, :] = value[23:24]
        src1[slot, 32:33, :] = value[0:1]

    def coarse_rows(slot):
        return [src1[slot, pl.ds(8 + start, MSG, stride=2), :] for start in (0, 1, -1, 2)]

    lane16 = lanes(MSG)
    place16 = (lane16 + 2 * odd) & 3

    def level2_parts(have, planes):
        parts = {}
        for d in planes:
            pair = [coarse_rows(q + 4) for q in (2 * d, 2 * d + 1) if q in have]
            beyond = [coarse_rows(q + 4) for q in (2 * d - 1, 2 * d + 2) if q in have]
            parts[d] = restricted(pair, beyond, [], KEEP, SIDE[1], 2)
        return parts

    def laid(parts, planes):
        by_place = {d % 4: parts[d] for d in planes}
        return jnp.where(place16 < 2, jnp.where(place16 == 0, by_place[0], by_place[1]), jnp.where(place16 == 2, by_place[2], by_place[3]))

    slot1 = pl.ds(pl.multiple_of((s + 1) * MSG, MSG), MSG)
    slot2 = pl.ds(pl.multiple_of((s + 2) * MSG2, MSG2), MSG2)

    def send_first(parts):
        gather[slot1, :] = laid(parts, range(-1, 3))

        @pl.when(core == 1)
        def _():
            pl.semaphore_wait(go, 1)

        for peer in peers:
            remote(gather.at[slot1], gather.at[slot1], gat_send.at[0], gat_recv.at[0], at_slab(peer)).start()

    def send_second(parts):
        msg2[0:12, :] = laid(parts, range(-1, 3))[0:12]
        msg2[12:24, :] = laid(parts, (-3, -2, 3, 4))[0:12]
        gather2[slot2, :] = msg2[...]
        for peer in peers:
            remote(msg2, gather2.at[slot2], gat_send.at[1], gat_recv.at[1], at_slab(peer)).start()

    def gathered(g):
        most = gather.at[pl.ds(0, (n_slab - 1) * MSG)] if g == 0 else gather2.at[pl.ds(0, (n_slab - 1) * MSG2)]
        return remote(most, most, gat_send.at[g], gat_recv.at[g], at_slab(above))

    row8 = lax.broadcasted_iota(jnp.int32, (8, 128), 0)
    lane8 = lanes(8)
    first_row, last_row = row8 == 0, row8 == 7

    def level2_sides(u):
        result = []
        for y in range(12):
            here = u[y]
            up = jnp.where(last_row, 0.0, turn(turn(here, 3, 1), -1, 0))
            down = jnp.where(first_row, 0.0, turn(turn(here, -3, 1), 1, 0))
            up = jnp.where((lane8 & 3) == 3, up, turn(here, -1, 1))
            down = jnp.where((lane8 & 3) == 0, down, turn(here, 1, 1))
            x = turn(here, 4, 1) + turn(here, -4, 1)
            result.append(total([u[(y + 1) % 12], u[(y + 11) % 12], up, down, x]))
        return result

    def level3_sides(u):
        result = []
        lower = (lane8 & 2) == 0
        for y in range(6):
            here = u[y]
            a, b = turn(here, -2, 1), turn(here, 2, 1)
            far = jnp.where(lower, jnp.where(first_row, 0.0, turn(a, 1, 0)), jnp.where(last_row, 0.0, turn(b, -1, 0)))
            x = turn(here, 8, 1) + turn(here, -8, 1)
            result.append(total([u[(y + 1) % 6], u[(y + 5) % 6], jnp.where(lower, a, b), far, x]))
        return result

    place8 = lane8 & 3

    def first_source():
        source = []
        for y in range(12):
            even, odd_, even_after, odd_before = [gather[pl.ds(MSG * k + y, 8, stride=2 * MSG), :] for k in (1, 2, 3, 0)]
            source.append(jnp.where(place8 == 3, even_after, even) + jnp.where(place8 == 0, odd_before, odd_))
        return source

    def second_source():
        source = []
        for y in range(12):
            even, odd_, even_after, odd_before = [gather2[pl.ds(MSG2 * k + y, 8, stride=2 * MSG2), :] for k in (2, 3, 4, 1)]
            near = jnp.where(place8 == 3, even_after, even) + jnp.where(place8 == 0, odd_before, odd_)
            even_before, even, even_after, odd_before, odd_, odd_after = [
                gather2[pl.ds(MSG2 * k + 12 + y, 8, stride=2 * MSG2), :] for k in (0, 2, 4, 1, 3, 5)]
            far = jnp.where(place8 == 0, even_before, jnp.where(place8 == 3, even, even_after))
            far = far + jnp.where(place8 == 0, odd_, jnp.where(place8 == 3, odd_after, odd_before))
            source.append(near + far)
        return source

    def response(u):
        weights = response_weights()
        plane = 4 * row8 + place8

        def weight(dz, dy, dx):
            inner = float(weights[4, dz + 2, dy, dx])
            value = inner
            for at, z in ((0, 0), (1, 1), (30, 6), (31, 7)):
                if abs(weights[z, dz + 2, dy, dx] - inner) > 1e-12:
                    value = jnp.where(plane == at, jnp.float32(weights[z, dz + 2, dy, dx]), value)
            return value

        x1 = [turn(a, 4, 1) + turn(a, -4, 1) for a in u]
        x2 = [turn(a, 8, 1) + turn(a, -8, 1) for a in u]

        def beside(a, y, by):
            return a[(y + by) % 12] + a[(y - by) % 12]

        groups = ((0, 0), (0, 1), (0, 2), (1, 1), (1, 2))
        by_dz = {dz: [weight(dz, *group) for group in groups] for dz in (-1, 0, 1)}
        two = [float(weights[4, 4, dy, dx]) for dy, dx in ((0, 0), (0, 1), (1, 1))]
        result = []
        for y in range(12):
            sums = [u[y], x1[y] + beside(u, y, 1), x2[y] + beside(u, y, 2), beside(x1, y, 1), beside(x2, y, 1) + beside(x1, y, 2)]
            here, up, down = [total([w * a for w, a in zip(by_dz[dz], sums)]) for dz in (0, -1, 1)]
            far = two[0] * sums[0] + two[1] * sums[1] + two[2] * sums[3]
            up = jnp.where(place8 == 3, jnp.where(last_row, 0.0, turn(turn(up, 3, 1), -1, 0)), turn(up, -1, 1))
            down = jnp.where(place8 == 0, jnp.where(first_row, 0.0, turn(turn(down, -3, 1), 1, 0)), turn(down, 1, 1))
            a, b = turn(far, 2, 1), turn(far, -2, 1)
            far = jnp.where(place8 >= 2, a + jnp.where(last_row, 0.0, turn(a, -1, 0)), b + jnp.where(first_row, 0.0, turn(b, 1, 0)))
            result.append(total([here, up, down, far]))
        return result

    def solve_level2(source):
        sides = level2_sides(source)
        residual = [KEEP * a + SIDE[2] * b for a, b in zip(source, sides)]
        source3 = []
        for y in range(6):
            pair = residual[2 * y] + residual[2 * y + 1]
            pair = pair + swapped(pair, 1)
            source3.append(0.125 * (pair + swapped(pair, 4)))
        pull = [PULL[3] * a for a in source3]
        iterate = pull
        for _ in range(SWEEPS - 1):
            sides = level3_sides(iterate)
            iterate = [KEEP * a + b + SIDE[3] * c for a, b, c in zip(iterate, pull, sides)]
        pull = [PULL[2] * a for a in source]
        u = [a + iterate[y // 2] for y, a in enumerate(pull)]
        sides = level2_sides(u)
        return [KEEP * a + b + SIDE[2] * c for a, b, c in zip(u, pull, sides)]

    def spread_level2(g, ds):
        row = 8 + s // 2
        a, b, c = [(e2, e2b)[g][pl.ds(row + by, MSG, stride=24), :] for by in (-1, 0, 1)]
        for d in ds:
            rows = a if d == -3 else jnp.where(odd == 1, b, a) if d < 0 else b if d < 2 else jnp.where(odd == 1, c, b) if d < 4 else c
            value = jnp.where(place16 == d % 4, rows, 0.0)
            value = value + swapped(value, 1)
            value = value + swapped(value, 2)
            pe2[g, d + 3, pl.ds(0, MSG, stride=2), :] = value
            pe2[g, d + 3, pl.ds(1, MSG, stride=2), :] = value

    even24 = (lanes(24) & 1) == 0

    def packed(a, b):
        return jnp.where(even24, a, b)

    def unpacked(value):
        return jnp.where(even24, value, turn(value, 1, 1)), jnp.where(even24, turn(value, -1, 1), value)

    def put_pe1(q, value):
        pe1[q + 4, pl.ds(8, 24, stride=2), :] = value
        pe1[q + 4, pl.ds(9, 24, stride=2), :] = value
        pe1[q + 4, 7:8, :] = value[23:24]
        pe1[q + 4, 56:57, :] = value[0:1]

    def correct_level1(g, reach):
        u = {q: pe2[g, q // 2 + 3, 0:24, :] for q in range(-reach - 1, 5 + reach)}
        return {
            q: KEEP * u[q] + (SIDE[1] * inside(q, 4)) * total([u[q - 1], u[q + 1], in_plane(u[q], 2)])
            for q in range(-reach, 4 + reach)
        }

    def base_level1(planes):
        answer = {}
        for q in planes:
            here = PULL[1] * f1[q + 3]
            sides = total([PULL[1] * f1[q + 2], PULL[1] * f1[q + 4], in_plane(here, 2)])
            answer[q] = (KEEP + 1.0) * here + (SIDE[1] * inside(q, 4)) * sides
        return answer

    def smooth(at, planes, plane, source):
        flag = inside(plane, 8)
        near = [at(p)[0] for p in (plane - 1, plane + 1) if p in planes]
        terms = []
        if plane in planes:
            here, before, after = at(plane)
            near += [before, after, turn(here, 1, 1) + turn(here, -1, 1)]
            terms.append(KEEP * here)
        if plane in source:
            terms.append((PULL[0] * flag) * f[plane + 3, 8:56, :])
        return total(terms + [(SIDE[0] * flag) * total(near)])

    def rows_at(ref, slot):
        return ref[slot, 8:56, :], ref[slot, 7:55, :], ref[slot, 9:57, :]

    def at_v2(p):
        return rows_at(v2, p + 4)

    def at_v(p):
        return rows_at(v, p + 6)

    def at_v1(p):
        return rows_at(v1, p + 6)

    def at_coarse(p):
        return rows_at(pe1, p // 2 + 4)

    def smooth_coarse(q):
        here, before, after = at_coarse(2 * q)
        side = SIDE[0] * inside(q, 4)
        inner = KEEP * here + side * total([here, before, after, turn(here, 1, 1), turn(here, -1, 1)])
        return inner + side * at_coarse(2 * q - 2)[0], inner + side * at_coarse(2 * q + 2)[0]

    def residual_mean(q, planes, source):
        pair = [fine_rows(v1, p + 6) for p in (2 * q, 2 * q + 1) if p in planes]
        beyond = [fine_rows(v1, p + 6) for p in (2 * q - 1, 2 * q + 2) if p in planes]
        rows = [fine_rows(f, p + 3)[:2] for p in (2 * q, 2 * q + 1) if p in source]
        return restricted(pair, beyond, rows, -CENTRE[0], STEP[0], 1)

    slab = range(8)
    for q in range(-1, 5):
        pair = [fine_rows(f, p + 3) for p in (2 * q, 2 * q + 1) if p in slab]
        beyond = [fine_rows(f, p + 3) for p in (2 * q - 1, 2 * q + 2) if p in slab]
        put_src1(q + 4, restricted(pair, beyond, [], KEEP, SIDE[0] * inside(q, 4), 1))
    send_first(level2_parts(range(-1, 5), range(-1, 3)))
    parts = {q: src1[q + 4, 8:32, :] for q in range(-1, 5)}
    for i in range(3):
        f1_out[i] = packed(parts[2 * i - 1], parts[2 * i])
    @pl.when(leads)
    def _():
        for copy in to_before:
            copy.start()

    @pl.when((core == 0) & (o != 0))
    def _():
        orb_n[...] = orb_x[...]
        occ_n[...] = occ_x[...]

    @pl.when(start)
    def _():
        orb_n[...] = orb_y[...]
        occ_n[...] = occ_y[...]

    below2, above2 = lax.rem(s + n_slab - 2, n_slab), lax.rem(s + 2, n_slab)
    send(f1_out.at[pl.ds(0, 2)], f1_in.at[pl.ds(2, 2)], f1_send.at[0], f1_recv.at[0], at_slab(below))
    send(f1_out.at[pl.ds(1, 2)], f1_in.at[pl.ds(0, 2)], f1_send.at[1], f1_recv.at[1], at_slab(above))

    send(f.at[pl.ds(3, 3), pl.ds(8, NY)], f.at[pl.ds(11, 3), pl.ds(8, NY)], f_send.at[0], f_recv.at[0], at_slab(below))
    send(f.at[pl.ds(8, 3), pl.ds(8, NY)], f.at[pl.ds(0, 3), pl.ds(8, NY)], f_send.at[1], f_recv.at[1], at_slab(above))
    faces = pending[2:4]
    pulled = {q: PULL[1] * parts[q] for q in parts}
    for q in range(-2, 6):
        near = [pulled.get(q - 1), pulled.get(q + 1)]
        terms = []
        if q in parts:
            near.append(in_plane(pulled[q], 2))
            terms = [(KEEP + 1.0) * pulled[q]]
        put_pe1(q, total(terms + [(SIDE[1] * inside(q, 4)) * total(near)]))
    for p in range(-4, 12):
        put(v2, p + 4, PULL[0] * f[p + 3, 8:56, :] + at_coarse(p)[0] if p in slab else at_coarse(p)[0])
    for p in range(-5, 13):
        put(v, p + 6, smooth(at_v2, range(-4, 12), p, slab))
    for p in range(-6, 14):
        put(v1, p + 6, smooth(at_v, range(-5, 13), p, slab))
    for q in range(-4, 8):
        put_src1(q + 4, inside(q, 4) * residual_mean(q, range(-6, 14), slab))
    shares = {q: src1[q + 4, 8:32, :] for q in (-4, -3, -2, -1, 2, 3, 0, 1, 4, 5, 6, 7)}
    for i, q in enumerate((-4, 0, 2, 6)):
        f2_out[i] = packed(shares[q], shares[q + 1])
    for i, device in enumerate((below2, below, above, above2)):
        send(f2_out.at[i], f2_in.at[i], f1_send.at[2 + i], f1_recv.at[2 + i], at_slab(device))
    send_second(level2_parts(range(-4, 8), range(-3, 5)))

    pending[0].wait_recv()
    pending[1].wait_recv()
    under = [low * plane for i in range(2) for plane in unpacked(f1_in[i])]
    over = [high * plane for i in range(2, 4) for plane in unpacked(f1_in[i])]
    mixed = {q: [part] for q, part in parts.items()}
    for first_plane, planes in ((-3, under), (3, over)):
        for i, plane in enumerate(planes):
            mixed.setdefault(first_plane + i, []).append(plane)
    for q in range(-3, 7):
        f1[q + 3] = total(mixed[q])
    base = base_level1(range(-2, 6))
    for q in base:
        e1[q + 2] = base[q]

    gathered(0).wait_recv()
    first = solve_level2(first_source())
    for y in range(12):
        e2[24 * y + 8 : 24 * y + 16, :] = first[y]
    answer = response(first)
    spread_level2(0, range(-3, 5))
    answer1 = correct_level1(0, 4)
    for q in range(-2, 6):
        put_pe1(q, answer1[q] + e1[q + 2])
    for face in faces:
        face.wait_recv()
    for p in range(-3, 11):
        put(v2, p + 4, (PULL[0] * inside(p, 8)) * f[p + 3, 8:56, :] + at_coarse(p)[0])
    for p in range(-2, 10):
        put(v, p + 6, smooth(at_v2, range(-3, 11), p, range(-3, 11)))
    for p in range(-1, 9):
        put(v1, p + 6, smooth(at_v, range(-2, 10), p, range(-3, 11)))
    weight_x = -occ_x[0:1, :]
    to_x = []
    for h in range(4):
        for p in range(2 * h, 2 * h + 2):
            last[p] = smooth(at_v1, range(-1, 9), p, slab)
            both_x[0, p] = (last[p] * weight_x) * orb_x[p]
        planes = pl.ds(2 * h, 2)
        to_x.append(remote(both_x.at[0, planes], both_x.at[1, planes], prev_send.at[h], prev_recv.at[h], before))

        @pl.when(leads)
        def _():
            to_x[h].start()

    @pl.when(start)
    def _():
        weight_y = -occ_y[0:1, :]
        for p in range(8):
            both_x[1, p] = (last[p] * weight_y) * orb_y[p]

    for q in range(4):
        f1[q + 3] = residual_mean(q, range(-1, 9), slab)

    for copy in pending[4:8]:
        copy.wait_recv()
    gathered(1).wait_recv()
    second = solve_level2([a + b for a, b in zip(answer, second_source())])
    for y in range(12):
        e2b[24 * y + 8 : 24 * y + 16, :] = second[y]
    for q in answer1:
        put_pe1(q, answer1[q])
    for lowest in (-6, 6):
        for q in range(lowest // 2, lowest // 2 + 4):
            for p, plane in zip((2 * q, 2 * q + 1), smooth_coarse(q)):
                put(v, p + 6, plane)
        for p in range(lowest + 1, lowest + 7):
            put(v1, p + 6, smooth(at_v, range(lowest, lowest + 8), p, ()))
    own_part = {q: inside(q, 4) * residual_mean(q, range(-6, 14), ()) for q in (-2, -1, 4, 5)}
    for q, near, far, near_flag, far_flag in ((-2, 2, 3, low, low2), (4, 1, 0, high, high2)):
        for i, (a, b) in enumerate(zip(unpacked(f2_in[near]), unpacked(f2_in[far]))):
            f1[q + i + 3] = total([shares[q + i], own_part[q + i], near_flag * a, far_flag * b])
    spread_level2(1, range(-1, 3))
    answer1 = correct_level1(1, 1)
    base = base_level1(range(-1, 5))
    fixes = {q: answer1[q] + base[q] for q in answer1}
    for i in range(3):
        fix_out[i] = packed(fixes[2 * i - 1], fixes[2 * i])
    fix_copy = remote(fix_out, fix_in, before_send.at[2], before_recv.at[2], before)

    @pl.when(leads)
    def _():
        fix_copy.start()

    @pl.when(core == 0)
    def _():
        fix_in[...] = fix_out[...]

    for q in fixes:
        put_pe1(q, fixes[q])

    weight_y = -occ_y[0:1, :]
    to_y = []
    for h in range(4):
        for p, fix in zip((2 * h, 2 * h + 1), smooth_coarse(h)):
            potential = last[p] + fix
            out_y[p] = (potential * weight_y) * orb_y[p]

            @pl.when(home)
            def _():
                in_y[p] = (potential * weight_x) * orb_x[p]

        planes = pl.ds(2 * h, 2)
        to_y.append(remote(out_y.at[planes], in_y.at[planes], ret_send.at[h], ret_recv.at[h], partner))

        @pl.when(jnp.logical_not(start))
        def _():
            to_y[h].start()

    @pl.when(core == 1)
    def _():
        for copy in to_before + to_x:
            copy.wait_recv()
        fix_copy.wait_recv()

    for i in range(3):
        for q, plane in zip((2 * i - 1, 2 * i), unpacked(fix_in[i])):
            put_pe1(q, plane)
    weight_n = -occ_n[0:1, :]
    kept = jnp.where(start, 1, core)
    for h in range(4):
        for p, fix in zip((2 * h, 2 * h + 1), smooth_coarse(h)):
            both_x[kept, p] = both_x[kept, p] + (fix * weight_n) * orb_n[p]
    for h in range(4):

        @pl.when(jnp.logical_not(home))
        def _():
            to_y[h].wait_recv()

        for p in range(2 * h, 2 * h + 2):
            out_ref[0, p] = in_y[p] + both_x[kept, p]

    for copy in pending:
        copy.wait_send()

    @pl.when(jnp.logical_not(home))
    def _():
        for copy in to_partner:
            copy.wait_send()

    @pl.when(jnp.logical_not(start))
    def _():
        for copy in to_y:
            copy.wait_send()

    for g in range(2):
        gathered(g).wait_send()

    @pl.when(core == 1)
    def _():
        for copy in to_next:
            copy.wait_send()

    @pl.when(leads)
    def _():
        for copy in to_x + to_before + [fix_copy]:
            copy.wait_send()


def on_device(n_orb, n_slab, orbitals, occupations):
    vmem, dma = pltpu.VMEM, pltpu.SemaphoreType.DMA
    f32 = jnp.float32

    def fine(planes):
        return vmem((planes, NY, NX), f32)

    def tall(planes):
        return vmem((planes, FINE, NX), f32)

    return pl.pallas_call(
        functools.partial(kernel, n_orb, n_slab),
        out_shape=jax.ShapeDtypeStruct(orbitals.shape, f32),
        in_specs=[pl.BlockSpec(memory_space=pltpu.SMEM), pl.BlockSpec(memory_space=pltpu.HBM)],
        out_specs=pl.BlockSpec(memory_space=pltpu.VMEM),
        scratch_shapes=[
            fine(8), fine(8), fine(8), vmem((8, 128), f32), vmem((8, 128), f32), vmem((8, 128), f32),
            tall(14), tall(16), tall(20), tall(20), tall(12),
            vmem((10, 24, 128), f32), vmem((12, ROWS1, 128), f32), vmem((2, 8, 40, 128), f32), vmem((8, 24, 128), f32),
            vmem((3, 24, 128), f32), vmem((4, 24, 128), f32), vmem((4, 24, 128), f32), vmem((4, 24, 128), f32), vmem((MSG2, 128), f32),
            vmem((20 * MSG, 128), f32), vmem((22 * MSG2, 128), f32), vmem((24 * 17, 128), f32), vmem((24 * 17, 128), f32),
            fine(8), fine(8), vmem((2, 8, NY, NX), f32),
            fine(8), vmem((8, 128), f32), fine(8), vmem((3, 24, 128), f32), vmem((3, 24, 128), f32),
            pltpu.SemaphoreType.REGULAR, dma, dma((2,)), dma((2,)), dma((2,)), dma((2,)), dma((2,)), dma((2,)), dma((6,)), dma((6,)), dma((2,)), dma((2,)),
            dma((4,)), dma((4,)), dma((4,)), dma((4,)), dma((3,)), dma((3,)),
        ],
        compiler_params=pltpu.CompilerParams(collective_id=0, has_side_effects=True, vmem_limit_bytes=32 * 2**20),
    )(occupations, pltpu.with_memory_space_constraint(orbitals, pltpu.HBM))


def solution(mesh):
    return jax.shard_map(
        functools.partial(on_device, mesh.shape["orb"], mesh.shape["slab"]),
        mesh=mesh,
        in_specs=(P("orb", "slab", None, None), P("orb")),
        out_specs=P("orb", "slab", None, None),
        check_vma=False,
    )
```

```python
import functools

import jax
import jax.numpy as jnp
import numpy as np
from jax import lax
from jax.experimental import pallas as pl
from jax.experimental.pallas import tpu as pltpu
from jax.sharding import PartitionSpec as P

MESH = pl.DeviceIdType.MESH

NZ, NY, NX = 128, 48, 128
SWEEPS = 6
screening = 0.001
relaxation = 0.8

STEP = [0.25**level for level in range(4)]
CENTRE = [6.0 * step + screening for step in STEP]
KEEP = 1.0 - relaxation
PULL = [relaxation / centre for centre in CENTRE]
SIDE = [pull * step for pull, step in zip(PULL, STEP)]

ROWS1 = 48
FINE = 64
MSG = 16
MSG2 = 24


def response_weights():
    def sides(u):
        padded = np.pad(u, ((0, 0), (1, 1), (0, 0), (0, 0)))
        return padded[:, 2:] + padded[:, :-2] + sum(np.roll(u, by, axis) for by in (1, -1) for axis in (2, 3))

    def smoothed(u, level):
        return KEEP * u + SIDE[level] * sides(u)

    def mean(u):
        b, z, y, x = u.shape
        return u.reshape(b, z // 2, 2, y // 2, 2, x // 2, 2).mean((2, 4, 6))

    def spread(u):
        return u.repeat(2, 1).repeat(2, 2).repeat(2, 3)

    unit = np.zeros((8, 8, 6, 6))
    for z in range(8):
        unit[z, z, 0, 0] = 1.0
    u = spread(smoothed(spread(unit), 1))
    u = smoothed(smoothed(u, 0), 0)
    u = mean(STEP[0] * sides(u) - CENTRE[0] * u)
    u = mean(smoothed(u, 1))
    weights = np.zeros((8, 5, 3, 3))
    for z in range(8):
        for dz in range(-2, 3):
            if 0 <= z + dz < 8:
                weights[z, dz + 2] = u[z, z + dz, :3, :3]
    return weights


def turn(value, by, axis):
    return pltpu.roll(value, by % value.shape[axis], axis)


def put(ref, slot, value):
    ref[slot, 8:56, :] = value
    ref[slot, 7:8, :] = value[47:48]
    ref[slot, 56:57, :] = value[0:1]


def lanes(rows):
    return lax.broadcasted_iota(jnp.int32, (rows, 128), 1)


def in_plane(value, lane_step):
    return (turn(value, 1, 0) + turn(value, -1, 0)) + (turn(value, lane_step, 1) + turn(value, -lane_step, 1))


def swapped(value, bit):
    first = (lanes(value.shape[0]) & bit) == 0
    return jnp.where(first, turn(value, -bit, 1), turn(value, bit, 1))


def total(parts):
    parts = [part for part in parts if part is not None]
    while len(parts) > 1:
        parts = [a + b for a, b in zip(parts[::2], parts[1::2])] + parts[len(parts) // 2 * 2 :]
    return parts[0] if parts else None


def kernel(
    n_orb, n_slab,
    occ_ref, orb_ref, out_ref,
    own, orb_x, orb_y, occ_own, occ_x, occ_y, f, v2, v, v1, pe1, f1, src1, pe2, e1, f1_out, f1_in, f2_out, f2_in, msg2, gather, gather2, e2, e2b,
    out_y, in_y, both_x, orb_n, occ_n, last, fix_out, fix_in,
    go, local_sem, orb_send, orb_recv, next_send, next_recv, gat_send, gat_recv, f1_send, f1_recv, f_send, f_recv, ret_send, ret_recv, prev_send, prev_recv, before_send, before_recv,
):
    o, s = lax.axis_index("orb"), lax.axis_index("slab")
    core = lax.rem(o, 2)
    partner = {"orb": o + 1 - 2 * core}
    before = {"orb": lax.rem(o + n_orb - 1 - core, n_orb)}
    after = {"orb": lax.rem(o + 2 - o // (n_orb - 1), n_orb)}
    start, home = o == 0, o == 1
    leads = (core == 1) & (o != 1) | (o == 0)
    above, below = lax.rem(s + 1, n_slab), lax.rem(s + n_slab - 1, n_slab)
    odd = lax.rem(s, 2)

    def at_slab(index):
        return {"slab": index}

    mine = pltpu.make_async_copy(orb_ref.at[0], own, local_sem)
    mine.start()
    peers = sorted(((x, y) for x in range(4) for y in range(4) if x or y), key=lambda d: -min(d[0], 4 - d[0]) - min(d[1], 4 - d[1]))
    peers = [4 * lax.rem(s // 4 + y, 4) + lax.rem(s + x, 4) for x, y in peers]

    barrier = pltpu.get_barrier_semaphore()

    def greet(device):
        pl.semaphore_signal(barrier, inc=1, device_id=device, device_id_type=MESH)

    greet(partner)

    @pl.when(core == 0)
    def _():
        for peer in peers:
            greet({"orb": o, "slab": peer})

    @pl.when(leads)
    def _():
        greet(before)

    @pl.when(core == 1)
    def _():
        greet({"orb": lax.rem(o + 1, n_orb)})
        for peer in peers:
            greet({"orb": o - 1, "slab": peer})

    occ_own[...] = jnp.full((8, 128), occ_ref[0], jnp.float32)
    for slot in (0, 17):
        gather[pl.ds(slot * MSG, MSG), :] = jnp.zeros((MSG, 128), jnp.float32)
    for slot in (0, 18):
        gather2[pl.ds(slot * MSG2, 2 * MSG2), :] = jnp.zeros((2 * MSG2, 128), jnp.float32)
    e2[...] = jnp.zeros_like(e2)
    e2b[...] = jnp.zeros_like(e2b)
    src1[...] = jnp.zeros_like(src1)
    low = jnp.where(s > 0, 1.0, 0.0).astype(jnp.float32)
    high = jnp.where(s < n_slab - 1, 1.0, 0.0).astype(jnp.float32)
    low2 = jnp.where(s > 1, 1.0, 0.0).astype(jnp.float32)
    high2 = jnp.where(s < n_slab - 2, 1.0, 0.0).astype(jnp.float32)

    def inside(plane, count):
        return low if plane < 0 else high if plane >= count else 1.0

    def remote(src, dst, send_sem, recv_sem, device):
        return pltpu.make_async_remote_copy(src, dst, send_sem, recv_sem, device_id=device, device_id_type=MESH)

    mine.wait()

    @pl.when(core == 0)
    def _():
        pl.semaphore_wait(barrier, 2 * n_slab)
        pl.semaphore_signal(go, inc=1, device_id=partner, device_id_type=MESH)

    @pl.when(core == 1)
    def _():
        pl.semaphore_wait(barrier, 2)

    to_next = [
        remote(own, orb_y, next_send.at[0], next_recv.at[0], after),
        remote(occ_own, occ_y, next_send.at[1], next_recv.at[1], after),
    ]
    to_partner = [
        remote(own, orb_x, orb_send.at[0], orb_recv.at[0], partner),
        remote(occ_own, occ_x, orb_send.at[1], orb_recv.at[1], partner),
    ]

    @pl.when(core == 1)
    def _():
        for copy in to_next:
            copy.start()

    @pl.when(jnp.logical_not(home))
    def _():
        for copy in to_partner:
            copy.start()

    @pl.when(start)
    def _():
        occ_x[...] = occ_own[...]
        orb_x[...] = own[...]

    @pl.when(jnp.logical_not(leads))
    def _():
        occ_y[...] = occ_own[...]
        orb_y[...] = own[...]

    @pl.when(jnp.logical_not(start))
    def _():
        for copy in to_partner:
            copy.wait_recv()

    @pl.when(leads)
    def _():
        for copy in to_next:
            copy.wait_recv()

    for p in range(8):
        put(f, 3 + p, orb_x[p] * orb_y[p])

    to_before = [
        remote(orb_x, orb_n, before_send.at[0], before_recv.at[0], before),
        remote(occ_x, occ_n, before_send.at[1], before_recv.at[1], before),
    ]

    pending = []

    def send(src, dst, send_sem, recv_sem, device):
        copy = remote(src, dst, send_sem, recv_sem, device)
        copy.start()
        pending.append(copy)
        return copy

    def restricted(pair, beyond, source, centre, side, bit):
        beyond = total([part for plane in beyond for part in plane[:2]])
        terms = []
        if pair:
            even, odd_, before, after = [total([plane[i] for plane in pair]) for i in range(4)]
            both = even + odd_
            terms.append(centre * both)
            around = total([both + both, before, after, turn(both, bit, 1), turn(both, -bit, 1), beyond])
        else:
            around = beyond
        terms.append(side * around)
        terms += [part for plane in source for part in plane]
        mean = total(terms)
        return 0.125 * (mean + swapped(mean, bit))

    def fine_rows(ref, plane):
        return [ref[plane, pl.ds(8 + start, 24, stride=2), :] for start in (0, 1, -1, 2)]

    def put_src1(slot, value):
        src1[slot, 8:32, :] = value
        src1[slot, 7:8, :] = value[23:24]
        src1[slot, 32:33, :] = value[0:1]

    def coarse_rows(slot):
        return [src1[slot, pl.ds(8 + start, MSG, stride=2), :] for start in (0, 1, -1, 2)]

    lane16 = lanes(MSG)
    place16 = (lane16 + 2 * odd) & 3

    def level2_parts(have, planes):
        parts = {}
        for d in planes:
            pair = [coarse_rows(q + 4) for q in (2 * d, 2 * d + 1) if q in have]
            beyond = [coarse_rows(q + 4) for q in (2 * d - 1, 2 * d + 2) if q in have]
            parts[d] = restricted(pair, beyond, [], KEEP, SIDE[1], 2)
        return parts

    def laid(parts, planes):
        by_place = {d % 4: parts[d] for d in planes}
        return jnp.where(place16 < 2, jnp.where(place16 == 0, by_place[0], by_place[1]), jnp.where(place16 == 2, by_place[2], by_place[3]))

    slot1 = pl.ds(pl.multiple_of((s + 1) * MSG, MSG), MSG)
    slot2 = pl.ds(pl.multiple_of((s + 2) * MSG2, MSG2), MSG2)

    def send_first(parts):
        gather[slot1, :] = laid(parts, range(-1, 3))

        @pl.when(core == 1)
        def _():
            pl.semaphore_wait(go, 1)

        for peer in peers:
            remote(gather.at[slot1], gather.at[slot1], gat_send.at[0], gat_recv.at[0], at_slab(peer)).start()

    def send_second(parts):
        msg2[0:12, :] = laid(parts, range(-1, 3))[0:12]
        msg2[12:24, :] = laid(parts, (-3, -2, 3, 4))[0:12]
        gather2[slot2, :] = msg2[...]
        for peer in peers:
            remote(msg2, gather2.at[slot2], gat_send.at[1], gat_recv.at[1], at_slab(peer)).start()

    def gathered(g):
        most = gather.at[pl.ds(0, (n_slab - 1) * MSG)] if g == 0 else gather2.at[pl.ds(0, (n_slab - 1) * MSG2)]
        return remote(most, most, gat_send.at[g], gat_recv.at[g], at_slab(above))

    row8 = lax.broadcasted_iota(jnp.int32, (8, 128), 0)
    lane8 = lanes(8)
    first_row, last_row = row8 == 0, row8 == 7

    def level2_sides(u):
        result = []
        for y in range(12):
            here = u[y]
            up = jnp.where(last_row, 0.0, turn(turn(here, 3, 1), -1, 0))
            down = jnp.where(first_row, 0.0, turn(turn(here, -3, 1), 1, 0))
            up = jnp.where((lane8 & 3) == 3, up, turn(here, -1, 1))
            down = jnp.where((lane8 & 3) == 0, down, turn(here, 1, 1))
            x = turn(here, 4, 1) + turn(here, -4, 1)
            result.append(total([u[(y + 1) % 12], u[(y + 11) % 12], up, down, x]))
        return result

    def level3_sides(u):
        result = []
        lower = (lane8 & 2) == 0
        for y in range(6):
            here = u[y]
            a, b = turn(here, -2, 1), turn(here, 2, 1)
            far = jnp.where(lower, jnp.where(first_row, 0.0, turn(a, 1, 0)), jnp.where(last_row, 0.0, turn(b, -1, 0)))
            x = turn(here, 8, 1) + turn(here, -8, 1)
            result.append(total([u[(y + 1) % 6], u[(y + 5) % 6], jnp.where(lower, a, b), far, x]))
        return result

    place8 = lane8 & 3

    def first_source():
        source = []
        for y in range(12):
            even, odd_, even_after, odd_before = [gather[pl.ds(MSG * k + y, 8, stride=2 * MSG), :] for k in (1, 2, 3, 0)]
            source.append(jnp.where(place8 == 3, even_after, even) + jnp.where(place8 == 0, odd_before, odd_))
        return source

    def second_source():
        source = []
        for y in range(12):
            even, odd_, even_after, odd_before = [gather2[pl.ds(MSG2 * k + y, 8, stride=2 * MSG2), :] for k in (2, 3, 4, 1)]
            near = jnp.where(place8 == 3, even_after, even) + jnp.where(place8 == 0, odd_before, odd_)
            even_before, even, even_after, odd_before, odd_, odd_after = [
                gather2[pl.ds(MSG2 * k + 12 + y, 8, stride=2 * MSG2), :] for k in (0, 2, 4, 1, 3, 5)]
            far = jnp.where(place8 == 0, even_before, jnp.where(place8 == 3, even, even_after))
            far = far + jnp.where(place8 == 0, odd_, jnp.where(place8 == 3, odd_after, odd_before))
            source.append(near + far)
        return source

    def response(u):
        weights = response_weights()
        plane = 4 * row8 + place8

        def weight(dz, dy, dx):
            inner = float(weights[4, dz + 2, dy, dx])
            value = inner
            for at, z in ((0, 0), (1, 1), (30, 6), (31, 7)):
                if abs(weights[z, dz + 2, dy, dx] - inner) > 1e-12:
                    value = jnp.where(plane == at, jnp.float32(weights[z, dz + 2, dy, dx]), value)
            return value

        x1 = [turn(a, 4, 1) + turn(a, -4, 1) for a in u]
        x2 = [turn(a, 8, 1) + turn(a, -8, 1) for a in u]

        def beside(a, y, by):
            return a[(y + by) % 12] + a[(y - by) % 12]

        groups = ((0, 0), (0, 1), (0, 2), (1, 1), (1, 2))
        by_dz = {dz: [weight(dz, *group) for group in groups] for dz in (-1, 0, 1)}
        two = [float(weights[4, 4, dy, dx]) for dy, dx in ((0, 0), (0, 1), (1, 1))]
        result = []
        for y in range(12):
            sums = [u[y], x1[y] + beside(u, y, 1), x2[y] + beside(u, y, 2), beside(x1, y, 1), beside(x2, y, 1) + beside(x1, y, 2)]
            here, up, down = [total([w * a for w, a in zip(by_dz[dz], sums)]) for dz in (0, -1, 1)]
            far = two[0] * sums[0] + two[1] * sums[1] + two[2] * sums[3]
            up = jnp.where(place8 == 3, jnp.where(last_row, 0.0, turn(turn(up, 3, 1), -1, 0)), turn(up, -1, 1))
            down = jnp.where(place8 == 0, jnp.where(first_row, 0.0, turn(turn(down, -3, 1), 1, 0)), turn(down, 1, 1))
            a, b = turn(far, 2, 1), turn(far, -2, 1)
            far = jnp.where(place8 >= 2, a + jnp.where(last_row, 0.0, turn(a, -1, 0)), b + jnp.where(first_row, 0.0, turn(b, 1, 0)))
            result.append(total([here, up, down, far]))
        return result

    def solve_level2(source):
        sides = level2_sides(source)
        residual = [KEEP * a + SIDE[2] * b for a, b in zip(source, sides)]
        source3 = []
        for y in range(6):
            pair = residual[2 * y] + residual[2 * y + 1]
            pair = pair + swapped(pair, 1)
            source3.append(0.125 * (pair + swapped(pair, 4)))
        pull = [PULL[3] * a for a in source3]
        iterate = pull
        for _ in range(SWEEPS - 1):
            sides = level3_sides(iterate)
            iterate = [KEEP * a + b + SIDE[3] * c for a, b, c in zip(iterate, pull, sides)]
        pull = [PULL[2] * a for a in source]
        u = [a + iterate[y // 2] for y, a in enumerate(pull)]
        sides = level2_sides(u)
        return [KEEP * a + b + SIDE[2] * c for a, b, c in zip(u, pull, sides)]

    def spread_level2(g, ds):
        row = 8 + s // 2
        a, b, c = [(e2, e2b)[g][pl.ds(row + by, MSG, stride=24), :] for by in (-1, 0, 1)]
        for d in ds:
            rows = a if d == -3 else jnp.where(odd == 1, b, a) if d < 0 else b if d < 2 else jnp.where(odd == 1, c, b) if d < 4 else c
            value = jnp.where(place16 == d % 4, rows, 0.0)
            value = value + swapped(value, 1)
            value = value + swapped(value, 2)
            pe2[g, d + 3, pl.ds(0, MSG, stride=2), :] = value
            pe2[g, d + 3, pl.ds(1, MSG, stride=2), :] = value

    even24 = (lanes(24) & 1) == 0

    def packed(a, b):
        return jnp.where(even24, a, b)

    def unpacked(value):
        return jnp.where(even24, value, turn(value, 1, 1)), jnp.where(even24, turn(value, -1, 1), value)

    def put_pe1(q, value):
        pe1[q + 4, pl.ds(8, 24, stride=2), :] = value
        pe1[q + 4, pl.ds(9, 24, stride=2), :] = value
        pe1[q + 4, 7:8, :] = value[23:24]
        pe1[q + 4, 56:57, :] = value[0:1]

    def correct_level1(g, reach):
        u = {q: pe2[g, q // 2 + 3, 0:24, :] for q in range(-reach - 1, 5 + reach)}
        return {
            q: KEEP * u[q] + (SIDE[1] * inside(q, 4)) * total([u[q - 1], u[q + 1], in_plane(u[q], 2)])
            for q in range(-reach, 4 + reach)
        }

    def base_level1(planes):
        answer = {}
        for q in planes:
            here = PULL[1] * f1[q + 3]
            sides = total([PULL[1] * f1[q + 2], PULL[1] * f1[q + 4], in_plane(here, 2)])
            answer[q] = (KEEP + 1.0) * here + (SIDE[1] * inside(q, 4)) * sides
        return answer

    def smooth(at, planes, plane, source):
        flag = inside(plane, 8)
        near = [at(p)[0] for p in (plane - 1, plane + 1) if p in planes]
        terms = []
        if plane in planes:
            here, before, after = at(plane)
            near += [before, after, turn(here, 1, 1) + turn(here, -1, 1)]
            terms.append(KEEP * here)
        if plane in source:
            terms.append((PULL[0] * flag) * f[plane + 3, 8:56, :])
        return total(terms + [(SIDE[0] * flag) * total(near)])

    def rows_at(ref, slot):
        return ref[slot, 8:56, :], ref[slot, 7:55, :], ref[slot, 9:57, :]

    def at_v2(p):
        return rows_at(v2, p + 4)

    def at_v(p):
        return rows_at(v, p + 6)

    def at_v1(p):
        return rows_at(v1, p + 6)

    def at_coarse(p):
        return rows_at(pe1, p // 2 + 4)

    def residual_mean(q, planes, source):
        pair = [fine_rows(v1, p + 6) for p in (2 * q, 2 * q + 1) if p in planes]
        beyond = [fine_rows(v1, p + 6) for p in (2 * q - 1, 2 * q + 2) if p in planes]
        rows = [fine_rows(f, p + 3)[:2] for p in (2 * q, 2 * q + 1) if p in source]
        return restricted(pair, beyond, rows, -CENTRE[0], STEP[0], 1)

    slab = range(8)
    for q in range(-1, 5):
        pair = [fine_rows(f, p + 3) for p in (2 * q, 2 * q + 1) if p in slab]
        beyond = [fine_rows(f, p + 3) for p in (2 * q - 1, 2 * q + 2) if p in slab]
        put_src1(q + 4, restricted(pair, beyond, [], KEEP, SIDE[0] * inside(q, 4), 1))
    send_first(level2_parts(range(-1, 5), range(-1, 3)))
    parts = {q: src1[q + 4, 8:32, :] for q in range(-1, 5)}
    for i in range(3):
        f1_out[i] = packed(parts[2 * i - 1], parts[2 * i])
    @pl.when(leads)
    def _():
        for copy in to_before:
            copy.start()

    @pl.when((core == 0) & (o != 0))
    def _():
        orb_n[...] = orb_x[...]
        occ_n[...] = occ_x[...]

    @pl.when(start)
    def _():
        orb_n[...] = orb_y[...]
        occ_n[...] = occ_y[...]

    below2, above2 = lax.rem(s + n_slab - 2, n_slab), lax.rem(s + 2, n_slab)
    send(f1_out.at[pl.ds(0, 2)], f1_in.at[pl.ds(2, 2)], f1_send.at[0], f1_recv.at[0], at_slab(below))
    send(f1_out.at[pl.ds(1, 2)], f1_in.at[pl.ds(0, 2)], f1_send.at[1], f1_recv.at[1], at_slab(above))

    send(f.at[pl.ds(3, 3), pl.ds(8, NY)], f.at[pl.ds(11, 3), pl.ds(8, NY)], f_send.at[0], f_recv.at[0], at_slab(below))
    send(f.at[pl.ds(8, 3), pl.ds(8, NY)], f.at[pl.ds(0, 3), pl.ds(8, NY)], f_send.at[1], f_recv.at[1], at_slab(above))
    faces = pending[2:4]
    pulled = {q: PULL[1] * parts[q] for q in parts}
    for q in range(-2, 6):
        near = [pulled.get(q - 1), pulled.get(q + 1)]
        terms = []
        if q in parts:
            near.append(in_plane(pulled[q], 2))
            terms = [(KEEP + 1.0) * pulled[q]]
        put_pe1(q, total(terms + [(SIDE[1] * inside(q, 4)) * total(near)]))
    for p in range(-4, 12):
        put(v2, p + 4, PULL[0] * f[p + 3, 8:56, :] + at_coarse(p)[0] if p in slab else at_coarse(p)[0])
    for p in range(-5, 13):
        put(v, p + 6, smooth(at_v2, range(-4, 12), p, slab))
    for p in range(-6, 14):
        put(v1, p + 6, smooth(at_v, range(-5, 13), p, slab))
    for q in range(-4, 8):
        put_src1(q + 4, inside(q, 4) * residual_mean(q, range(-6, 14), slab))
    shares = {q: src1[q + 4, 8:32, :] for q in (-4, -3, -2, -1, 2, 3, 0, 1, 4, 5, 6, 7)}
    for i, q in enumerate((-4, 0, 2, 6)):
        f2_out[i] = packed(shares[q], shares[q + 1])
    for i, device in enumerate((below2, below, above, above2)):
        send(f2_out.at[i], f2_in.at[i], f1_send.at[2 + i], f1_recv.at[2 + i], at_slab(device))
    send_second(level2_parts(range(-4, 8), range(-3, 5)))

    pending[0].wait_recv()
    pending[1].wait_recv()
    under = [low * plane for i in range(2) for plane in unpacked(f1_in[i])]
    over = [high * plane for i in range(2, 4) for plane in unpacked(f1_in[i])]
    mixed = {q: [part] for q, part in parts.items()}
    for first_plane, planes in ((-3, under), (3, over)):
        for i, plane in enumerate(planes):
            mixed.setdefault(first_plane + i, []).append(plane)
    for q in range(-3, 7):
        f1[q + 3] = total(mixed[q])
    base = base_level1(range(-2, 6))
    for q in base:
        e1[q + 2] = base[q]

    gathered(0).wait_recv()
    first = solve_level2(first_source())
    for y in range(12):
        e2[24 * y + 8 : 24 * y + 16, :] = first[y]
    answer = response(first)
    spread_level2(0, range(-3, 5))
    answer1 = correct_level1(0, 4)
    for q in range(-2, 6):
        put_pe1(q, answer1[q] + e1[q + 2])
    for face in faces:
        face.wait_recv()
    for p in range(-3, 11):
        put(v2, p + 4, (PULL[0] * inside(p, 8)) * f[p + 3, 8:56, :] + at_coarse(p)[0])
    for p in range(-2, 10):
        put(v, p + 6, smooth(at_v2, range(-3, 11), p, range(-3, 11)))
    for p in range(-1, 9):
        put(v1, p + 6, smooth(at_v, range(-2, 10), p, range(-3, 11)))
    weight_x = -occ_x[0:1, :]
    to_x = []
    for h in range(4):
        for p in range(2 * h, 2 * h + 2):
            last[p] = smooth(at_v1, range(-1, 9), p, slab)
            both_x[0, p] = (last[p] * weight_x) * orb_x[p]
        planes = pl.ds(2 * h, 2)
        to_x.append(remote(both_x.at[0, planes], both_x.at[1, planes], prev_send.at[h], prev_recv.at[h], before))

        @pl.when(leads)
        def _():
            to_x[h].start()

    @pl.when(start)
    def _():
        weight_y = -occ_y[0:1, :]
        for p in range(8):
            both_x[1, p] = (last[p] * weight_y) * orb_y[p]

    for q in range(4):
        f1[q + 3] = residual_mean(q, range(-1, 9), slab)

    for copy in pending[4:8]:
        copy.wait_recv()
    gathered(1).wait_recv()
    second = solve_level2([a + b for a, b in zip(answer, second_source())])
    for y in range(12):
        e2b[24 * y + 8 : 24 * y + 16, :] = second[y]
    for q in answer1:
        put_pe1(q, answer1[q])
    for lowest in (-6, 6):
        for p in range(lowest, lowest + 8):
            put(v, p + 6, smooth(at_coarse, range(-8, 16), p, ()))
        for p in range(lowest + 1, lowest + 7):
            put(v1, p + 6, smooth(at_v, range(lowest, lowest + 8), p, ()))
    own_part = {q: inside(q, 4) * residual_mean(q, range(-6, 14), ()) for q in (-2, -1, 4, 5)}
    for q, near, far, near_flag, far_flag in ((-2, 2, 3, low, low2), (4, 1, 0, high, high2)):
        for i, (a, b) in enumerate(zip(unpacked(f2_in[near]), unpacked(f2_in[far]))):
            f1[q + i + 3] = total([shares[q + i], own_part[q + i], near_flag * a, far_flag * b])
    spread_level2(1, range(-1, 3))
    answer1 = correct_level1(1, 1)
    base = base_level1(range(-1, 5))
    fixes = {q: answer1[q] + base[q] for q in answer1}
    for i in range(3):
        fix_out[i] = packed(fixes[2 * i - 1], fixes[2 * i])
    fix_copy = remote(fix_out, fix_in, before_send.at[2], before_recv.at[2], before)

    @pl.when(leads)
    def _():
        fix_copy.start()

    @pl.when(core == 0)
    def _():
        fix_in[...] = fix_out[...]

    for q in fixes:
        put_pe1(q, fixes[q])

    weight_y = -occ_y[0:1, :]
    to_y = []
    for h in range(4):
        for p in range(2 * h, 2 * h + 2):
            potential = last[p] + smooth(at_coarse, range(-2, 10), p, ())
            out_y[p] = (potential * weight_y) * orb_y[p]

            @pl.when(home)
            def _():
                in_y[p] = (potential * weight_x) * orb_x[p]

        planes = pl.ds(2 * h, 2)
        to_y.append(remote(out_y.at[planes], in_y.at[planes], ret_send.at[h], ret_recv.at[h], partner))

        @pl.when(jnp.logical_not(start))
        def _():
            to_y[h].start()

    @pl.when(core == 1)
    def _():
        for copy in to_before + to_x:
            copy.wait_recv()
        fix_copy.wait_recv()

    for i in range(3):
        for q, plane in zip((2 * i - 1, 2 * i), unpacked(fix_in[i])):
            put_pe1(q, plane)
    weight_n = -occ_n[0:1, :]
    kept = jnp.where(start, 1, core)
    for p in range(8):
        both_x[kept, p] = both_x[kept, p] + (smooth(at_coarse, range(-2, 10), p, ()) * weight_n) * orb_n[p]
    for h in range(4):

        @pl.when(jnp.logical_not(home))
        def _():
            to_y[h].wait_recv()

        for p in range(2 * h, 2 * h + 2):
            out_ref[0, p] = in_y[p] + both_x[kept, p]

    for copy in pending:
        copy.wait_send()

    @pl.when(jnp.logical_not(home))
    def _():
        for copy in to_partner:
            copy.wait_send()

    @pl.when(jnp.logical_not(start))
    def _():
        for copy in to_y:
            copy.wait_send()

    for g in range(2):
        gathered(g).wait_send()

    @pl.when(core == 1)
    def _():
        for copy in to_next:
            copy.wait_send()

    @pl.when(leads)
    def _():
        for copy in to_x + to_before + [fix_copy]:
            copy.wait_send()


def on_device(n_orb, n_slab, orbitals, occupations):
    vmem, dma = pltpu.VMEM, pltpu.SemaphoreType.DMA
    f32 = jnp.float32

    def fine(planes):
        return vmem((planes, NY, NX), f32)

    def tall(planes):
        return vmem((planes, FINE, NX), f32)

    return pl.pallas_call(
        functools.partial(kernel, n_orb, n_slab),
        out_shape=jax.ShapeDtypeStruct(orbitals.shape, f32),
        in_specs=[pl.BlockSpec(memory_space=pltpu.SMEM), pl.BlockSpec(memory_space=pltpu.HBM)],
        out_specs=pl.BlockSpec(memory_space=pltpu.VMEM),
        scratch_shapes=[
            fine(8), fine(8), fine(8), vmem((8, 128), f32), vmem((8, 128), f32), vmem((8, 128), f32),
            tall(14), tall(16), tall(20), tall(20), tall(12),
            vmem((10, 24, 128), f32), vmem((12, ROWS1, 128), f32), vmem((2, 8, 40, 128), f32), vmem((8, 24, 128), f32),
            vmem((3, 24, 128), f32), vmem((4, 24, 128), f32), vmem((4, 24, 128), f32), vmem((4, 24, 128), f32), vmem((MSG2, 128), f32),
            vmem((20 * MSG, 128), f32), vmem((22 * MSG2, 128), f32), vmem((24 * 17, 128), f32), vmem((24 * 17, 128), f32),
            fine(8), fine(8), vmem((2, 8, NY, NX), f32),
            fine(8), vmem((8, 128), f32), fine(8), vmem((3, 24, 128), f32), vmem((3, 24, 128), f32),
            pltpu.SemaphoreType.REGULAR, dma, dma((2,)), dma((2,)), dma((2,)), dma((2,)), dma((2,)), dma((2,)), dma((6,)), dma((6,)), dma((2,)), dma((2,)),
            dma((4,)), dma((4,)), dma((4,)), dma((4,)), dma((3,)), dma((3,)),
        ],
        compiler_params=pltpu.CompilerParams(collective_id=0, has_side_effects=True, vmem_limit_bytes=32 * 2**20),
    )(occupations, pltpu.with_memory_space_constraint(orbitals, pltpu.HBM))


def solution(mesh):
    return jax.shard_map(
        functools.partial(on_device, mesh.shape["orb"], mesh.shape["slab"]),
        mesh=mesh,
        in_specs=(P("orb", "slab", None, None), P("orb")),
        out_specs=P("orb", "slab", None, None),
        check_vma=False,
    )
```
